512 devices in a mesh: row: 32 (over x, z_hi, core), col: 16 (over z_lo, y).
Axes of the slice: x: 4, y: 8, z: 8 (z_hi: 4, z_lo: 2; z = z_hi * 2 + z_lo), core: 2. Of those that a mesh axis runs over, the one named last changes fastest.
Arguments:
- embeddings: bfloat16 [65536, 128], P(('col', 'row')), may hold values from -6 to 6
- weight: bfloat16 [128, 256], replicated, may hold values from -0.5 to 0.5
- cotangent: bfloat16 [65536, 256], P(('row', 'col')), may hold values from -6 to 6
- adj_blocks: bfloat16 [32, 512, 4, 128, 128], P('row', 'col'), may hold values from -0.0625 to 0.0625
- block_rows: int32 [32, 512, 4], P('row', 'col'), may hold values from 0 to 15
- block_counts: int32 [32, 512], P('row', 'col'), may hold values from 0 to 4, as said below
Outputs:
- grad_embeddings: bfloat16 [65536, 128], P(('col', 'row'))
- grad_weight: float32 [128, 256], replicated
The draws below stay inside these ranges and needn't reach their ends.
Inputs may be any that keep to these rules, and one draw needn't show every extreme that they name: `block_counts`: counts differ from tile to tile; the first block column of each tile carries that tile's largest count, and some tile reaches 4.
All inputs are finite; a program needn't handle non-finite values.
Results may differ from the reference program's by a relative error of at most 0.02.
Values may be sent and summed in bfloat16 or wider, within the bound.
A program may use at most 64 MiB of HBM per device.

```python
import jax
import jax.numpy as jnp
from jax import lax

BLK = 128
F = 128
HID = 256
S = 4
BR = 16
NBC = 512
BC = 32
NODES = 65536
N_ROW = 32
N_COL = 16


def draw_block_counts(key, part):
    key = jax.random.fold_in(key, 7)
    level_key, count_key = jax.random.split(key)
    levels = jax.random.randint(level_key, (N_ROW, N_COL), 1, S + 1)
    tile_row = jnp.arange(N_ROW, dtype=jnp.int32)[:, None]
    tile_col = jnp.arange(N_COL, dtype=jnp.int32)[None, :]
    levels = jnp.where((tile_row == 0) & (tile_col == 0), S, levels)
    spread = jnp.repeat(levels, BC, axis=1)
    counts = jax.random.randint(count_key, (N_ROW, NBC), 0, spread + 1)
    first = jnp.arange(NBC, dtype=jnp.int32) % BC == 0
    return jnp.where(first[None, :], spread, counts).astype(jnp.int32)


def touch_ends(drawn, rng, low, largest):
    extent = drawn.shape
    place = [jax.random.randint(jax.random.fold_in(rng, axis), (), 0, extent[axis]) for axis in range(len(extent))]
    drawn = drawn.at[tuple(place)].set(low)
    longest = extent.index(max(extent))
    place[longest] = (place[longest] + 1) % extent[longest]
    return drawn.at[tuple(place)].set(largest)


def block_levels(stream_key, shape, pieces, smallest, high):
    factor_of = 1.0
    for axis_at, parts in pieces:
        steps = jax.random.uniform(jax.random.fold_in(jax.random.fold_in(stream_key, 6), axis_at), (parts,), jnp.float32, smallest / len(pieces), high / len(pieces))
        factor_of = factor_of * jnp.repeat(jnp.exp(steps), shape[axis_at] // parts).reshape((-1,) + (1,) * (len(shape) - 1 - axis_at))
    return factor_of


def scatter_about(key, shape, scale, reach, shards=(), kind=jnp.bfloat16):
    drawn = scale * jax.random.normal(key, shape, jnp.float32)
    if shards:
        drawn = drawn * block_levels(key, shape, shards, -0.22, 0.18)
    return jnp.clip(drawn, -reach, reach).astype(kind)


def setup_inputs(seed: int = 0) -> dict:
    arg_keys = jax.random.split(jax.random.key(seed), 7)
    return {
        "embeddings": scatter_about(arg_keys[0], (NODES, F), 1.0, 6.0, ((0, 512),)),
        "weight": scatter_about(arg_keys[1], (F, HID), F ** -0.5, 0.5),
        "cotangent": scatter_about(arg_keys[2], (NODES, HID), 1.0, 6.0, ((0, 512),)),
        "adj_blocks": scatter_about(arg_keys[3], (N_ROW, NBC, S, BLK, BLK), (BLK * NBC * S // (2 * BR)) ** -0.5, 0.0625, ((0, 32), (1, 16))),
        "block_rows": touch_ends(jax.random.randint(arg_keys[4], (N_ROW, NBC, S), 0, BR), jax.random.fold_in(arg_keys[4], 1), 0, BR - 1).astype(jnp.int32),
        "block_counts": draw_block_counts(jax.random.fold_in(arg_keys[6], 71), 0),
    }


def silu_slope(z):
    s = jax.nn.sigmoid(z)
    return s * (1.0 + z * (1.0 - s))


def reference(embeddings, weight, cotangent, adj_blocks, block_rows, block_counts):
    panels = embeddings.reshape(NBC, BLK, F).astype(jnp.float32)
    slot_ids = jnp.arange(S, dtype=jnp.int32)
    row_ids = jnp.arange(BR, dtype=jnp.int32)

    def forward_row(item):
        blocks, rows, counts = item
        live = slot_ids[None, :] < counts[:, None]
        select = ((rows[:, :, None] == row_ids[None, None, :]) & live[:, :, None]).astype(jnp.float32)
        prod = jnp.einsum("jsab,jbf->jsaf", blocks.astype(jnp.float32), panels)
        return jnp.einsum("jsk,jsaf->kaf", select, prod, precision=lax.Precision.HIGHEST)

    summed = lax.map(forward_row, (adj_blocks, block_rows, block_counts))
    aggregate = summed.reshape(NBC * BLK, F).astype(jnp.bfloat16)
    pre = jnp.dot(aggregate, weight, preferred_element_type=jnp.float32)
    dpre = (cotangent.astype(jnp.float32) * silu_slope(pre)).astype(jnp.bfloat16)
    grad_weight = jnp.dot(aggregate.T, dpre, preferred_element_type=jnp.float32)
    dagg = jnp.dot(dpre, weight.T, preferred_element_type=jnp.float32).astype(jnp.bfloat16)
    dagg_rows = dagg.reshape(N_ROW, BR, BLK, F)

    def backward_row(total, item):
        blocks, rows, counts, grads = item
        live = (slot_ids[None, :] < counts[:, None]).astype(jnp.float32)
        chosen = jnp.take(grads, rows, axis=0).astype(jnp.float32) * live[:, :, None, None]
        return total + jnp.einsum("jsba,jsbf->jaf", blocks.astype(jnp.float32), chosen), None

    total, unused = lax.scan(backward_row, jnp.zeros((NBC, BLK, F), jnp.float32),
                             (adj_blocks, block_rows, block_counts, dagg_rows))
    grad_embeddings = total.reshape(NBC * BLK, F).astype(jnp.bfloat16)
    return grad_embeddings, grad_weight
```

```python
import functools

import jax
import jax.numpy as jnp
from jax import lax
from jax.experimental import pallas as pl
from jax.experimental.pallas import tpu as pltpu
from jax.sharding import PartitionSpec as P

MESH = pl.DeviceIdType.MESH
BR = 16
NX, NZ, NY, NC = 4, 4, 8, 32
SLOTS = 4
B = 128
F = 128
HID = 256
NB = NC * SLOTS
BF = jnp.bfloat16
F32 = jnp.float32


def ring4(t):
    return 1 + 2 * t - 3 * (t // 2)


def kernel(
    idx, emb, wgt, cot, adj_hbm, gout, gw_out,
    adj, panel, prod, seg, zs, zr, ys, yr, dt, gt, cs, cr, keep, xs, xr, hs, hr,
    lw, lwr, ws, wr, w1, w1r, w2, w2r, w3, w3r, wg,
    sem_a, e_s, e_r, z_s, z_r, y_s, y_r, g_s, g_r, c_s, c_r, x_s, x_r, h_s, h_r,
    w_s, w_r,
):
    row = lax.axis_index("row")
    col = lax.axis_index("col")
    x, zh, core = row // 8, (row // 2) % NZ, row % 2
    zl, y = col // NY, col % NY

    def to_x(d):
        return ((((x + d) % NX) * NZ + zh) * 2 + core, col)

    def to_h(d):
        return ((x * NZ + (zh + d) % NZ) * 2 + core, col)

    def to_y(d):
        return (row, zl * NY + (y + d) % NY)

    sib = ((x * NZ + zh) * 2 + 1 - core, col)
    mate = (row, (1 - zl) * NY + y)

    def node(dx, dz, c):
        return (((x + dx) % NX) * NZ + (zh + dz) % NZ) * 2 + c

    def remote(src, dst, s, r, where):
        return pltpu.make_async_remote_copy(
            src_ref=src, dst_ref=dst, send_sem=s, recv_sem=r, device_id=where, device_id_type=MESH
        )

    loads = [
        pltpu.make_async_copy(adj_hbm.at[pl.ds(8 * q, 8)], adj.at[pl.ds(8 * q, 8)], sem_a.at[q])
        for q in range(4)
    ]
    for cp in loads:
        cp.start()

    barrier = pltpu.get_barrier_semaphore()
    peers = [sib, mate] + [to_x(d) for d in (1, 2, 3)] + [to_h(d) for d in (1, 2, 3)]
    peers += [to_y(d) for d in range(1, NY)]
    for peer in peers:
        pl.semaphore_signal(barrier, inc=1, device_id=peer, device_id_type=MESH)
    me = node(0, 0, core)
    gt[BR] = jnp.zeros((B, B), BF)
    seg[NB] = jnp.zeros((B, F), F32)
    panel[me] = emb[...]
    pl.semaphore_wait(barrier, len(peers))

    def spread(j, n, where, src=None):
        return remote(panel.at[j] if src is None else src, panel.at[j], e_s.at[n], e_r.at[j], where)

    for t, d in enumerate((1, 3, 2)):
        spread(me, t, to_h(d), emb).start()
    for t, d in enumerate((1, 3, 2)):
        spread(me, 3 + t, to_x(d), emb).start()
    spread(me, 6, sib, emb).start()

    def multiply(j):
        prod[pl.ds(j * SLOTS, SLOTS)] = jnp.dot(
            adj[j], panel[j], preferred_element_type=F32
        ).reshape(SLOTS, B, F)

    for cp in loads:
        cp.wait()
    multiply(me)

    def from_z(t, carry):
        j = node(0, ring4(t), core)
        spread(j, 0, sib).wait_recv()
        for q, d in enumerate((1, 3, 2)):
            spread(j, 7 + 4 * t + q, to_x(d)).start()
        spread(j, 7 + 4 * t + 3, sib).start()
        multiply(j)
        return carry

    lax.fori_loop(0, 3, from_z, 0)

    def from_x(t, carry):
        j = node(ring4(t % 3), (ring4(t // 3 - 1)) * jnp.minimum(t // 3, 1), core)
        spread(j, 0, sib).wait_recv()
        spread(j, 19 + t, sib).start()
        multiply(j)
        return carry

    lax.fori_loop(0, 12, from_x, 0)

    def from_sib(t, carry):
        j = node(t % NX, t // NX, 1 - core)
        spread(j, 0, sib).wait_recv()
        multiply(j)
        return carry

    lax.fori_loop(0, 16, from_sib, 0)

    def segment(i, total):
        total = prod[idx[i]] + total * idx[NB + i].astype(F32)
        seg[i] = total
        return total

    lax.fori_loop(0, NB, segment, jnp.zeros((B, F), F32))

    order = (4, 3, 5, 2, 6, 1, 7, 0)

    def part(half, d):
        return seg[idx[3 * NB + half * NY + (y + d) % NY]]

    def zcopy(d):
        return remote(zs.at[d], zr.at[d], z_s.at[d], z_r.at[d], mate)

    def ycopy(d):
        return remote(ys.at[d], yr.at[d], y_s.at[d], y_r.at[d], to_y(d))

    for d in order:
        zs[d] = part(1 - zl, d).astype(BF)
        zcopy(d).start()
    for d in order[:-1]:
        zcopy(d).wait_recv()
        ys[d] = (part(zl, d) + zr[d].astype(F32)).astype(BF)
        ycopy(d).start()
    zcopy(0).wait_recv()
    total = part(zl, 0) + zr[0].astype(F32)
    for d in (1, 7, 2, 6, 3, 5, 4):
        ycopy(d).wait_recv()
        total = total + yr[d].astype(F32)
    aggregate = total.astype(BF)

    weight = wgt[...]
    pre = jnp.dot(aggregate, weight, preferred_element_type=F32)
    s = 1.0 / (1.0 + jnp.exp(-pre))
    dpre = (cot[...].astype(F32) * (s * (1.0 + pre * (1.0 - s)))).astype(BF)
    dt[...] = lax.dot_general(
        weight, dpre, (((1,), (1,)), ((), ())), preferred_element_type=F32
    ).astype(BF)

    def share(k, n, where, src=None):
        return remote(gt.at[k] if src is None else src, gt.at[k], g_s.at[n], g_r.at[k], where)

    for d in order[:-1]:
        share(col, d, to_y(d), dt).start()
    share(col, 0, mate, dt).start()
    gt[col] = dt[...]

    lw[...] = lax.dot_general(
        aggregate, dpre, (((0,), (0,)), ((), ())), preferred_element_type=F32
    ).reshape(BR, 8, HID)
    w_first = remote(lw.at[pl.ds((1 - zl) * NY, NY)], lwr, w_s.at[0], w_r.at[0], mate)
    w_first.start()

    for d in (1, 7, 2, 6, 3, 5, 4):
        k = zl * NY + (y + d) % NY
        share(k, 0, mate).wait_recv()
        share(k, 7 + d, mate).start()

    w_first.wait_recv()

    def w_second(d):
        return remote(ws.at[d], wr.at[d], w_s.at[d], w_r.at[d], to_y(d))

    for d in range(1, NY):
        q = (y + d) % NY
        ws[d] = lw[zl * NY + q] + lwr[q]
        w_second(d).start()
    wtot = lw[zl * NY + y] + lwr[y]

    for d in (0, 1, 7, 2, 6, 3, 5, 4):
        share((1 - zl) * NY + (y + d) % NY, 0, mate).wait_recv()

    for d in range(1, NY):
        w_second(d).wait_recv()
        wtot = wtot + wr[d]
    w1[...] = wtot
    w_core = remote(w1, w1r, w_s.at[8], w_r.at[8], sib)
    w_core.start()

    def column_grad(j):
        picked = jnp.concatenate([gt[idx[2 * NB + j * SLOTS + q]] for q in range(SLOTS)], axis=1)
        return jnp.dot(picked, adj[j], preferred_element_type=F32)

    def ccopy(t):
        return remote(cs.at[t], cr.at[t], c_s.at[t], c_r.at[t], sib)

    def far(n):
        return (5 * n + 2 - (n // 2) * 8 + (n // 3) * 5) % 4

    def xcopy(t, d):
        return remote(xs.at[t], xr.at[t], x_s.at[t], x_r.at[t], to_x(d))

    def produce(dz, dx):
        t = dz * NX + dx
        cs[t] = column_grad(node(dx, dz, 1 - core)).astype(BF)
        ccopy(t).start()
        keep[t] = column_grad(node(dx, dz, core))

    def pass_on(dz, dx):
        t = dz * NX + dx
        ccopy(t).wait_recv()
        both = keep[t] + cr[t].astype(F32)
        if dx == 0:
            keep[t] = both
        else:
            xs[t] = both.astype(BF)
            xcopy(t, dx).start()

    steps = [(dz, dx) for dz in (2, 1, 3, 0) for dx in (2, 1, 3, 0)]
    lag = 4
    for n in range(len(steps) + lag):
        if n < len(steps):
            produce(*steps[n])
        if n >= lag:
            pass_on(*steps[n - lag])

    w_core.wait_recv()
    first = jnp.where(core == 0, w1[...], w1r[...])
    second = jnp.where(core == 0, w1r[...], w1[...])
    w2[...] = first + second

    def w_x(d):
        return remote(w2, w2r.at[x], w_s.at[8 + d], w_r.at[8 + (NX - d) % NX], to_x(d))

    def w_x_recv(d):
        return remote(w2, w2r.at[(x + d) % NX], w_s.at[8 + d], w_r.at[8 + d], to_x(d))

    w2r[x] = w2[...]
    for d in (1, 3, 2):
        w_x(d).start()

    def hcopy(dz):
        return remote(hs.at[dz], hr.at[dz], h_s.at[dz], h_r.at[dz], to_h(dz))

    def w_h(d):
        return remote(w3, w3r.at[zh], w_s.at[11 + d], w_r.at[11 + (NZ - d) % NZ], to_h(d))

    def w_h_recv(d):
        return remote(w3, w3r.at[(zh + d) % NZ], w_s.at[11 + d], w_r.at[11 + d], to_h(d))

    def over_x(dz):
        acc = keep[dz * NX]
        for dx in (1, 3, 2):
            xcopy(dz * NX + dx, dx).wait_recv()
            acc = acc + xr[dz * NX + dx].astype(F32)
        return acc

    for dz in (2, 1):
        hs[dz] = over_x(dz).astype(BF)
        hcopy(dz).start()
    for d in (1, 3, 2):
        w_x_recv(d).wait_recv()
    w3[...] = (w2r[0] + w2r[1]) + (w2r[2] + w2r[3])
    w3r[zh] = w3[...]
    for d in (1, 3, 2):
        w_h(d).start()
    hs[3] = over_x(3).astype(BF)
    hcopy(3).start()
    acc = over_x(0)

    for d in (1, 3, 2):
        w_h_recv(d).wait_recv()
    wg[col] = (w3r[0] + w3r[1]) + (w3r[2] + w3r[3])

    def w_y(d):
        return remote(wg.at[col], wg.at[col], w_s.at[14 + d], w_r.at[14 + (NY - d) % NY], to_y(d))

    def w_y_recv(d):
        k = zl * NY + (y + d) % NY
        return remote(wg.at[k], wg.at[k], w_s.at[14 + d], w_r.at[14 + d], to_y(d))

    for d in order[:-1]:
        w_y(d).start()

    for dz in (1, 3, 2):
        hcopy(dz).wait_recv()
        acc = acc + hr[dz].astype(F32)
    gout[...] = acc.T.astype(BF)

    for d in (1, 7, 2, 6, 3, 5, 4):
        w_y_recv(d).wait_recv()
    w_last = remote(
        wg.at[pl.ds(zl * NY, NY)], wg.at[pl.ds(zl * NY, NY)], w_s.at[22], w_r.at[22], mate
    )
    w_last.start()

    for n in range(31):
        spread(me, n, sib).wait_send()
    for d in range(NY):
        zcopy(d).wait_send()
        if d:
            ycopy(d).wait_send()
    for n in range(15):
        share(col, n, mate).wait_send()
    for t in range(16):
        ccopy(t).wait_send()
        if t % NX:
            xcopy(t, 1).wait_send()
    for dz in (1, 2, 3):
        hcopy(dz).wait_send()
    w_first.wait_send()
    for d in range(1, NY):
        w_second(d).wait_send()
        w_y(d).wait_send()
    w_core.wait_send()
    for d in (1, 2, 3):
        w_x(d).wait_send()
        w_h(d).wait_send()
    w_last.wait()
    gw_out[...] = wg[...].reshape(F, HID)


def plan(rows, counts):
    live = jnp.arange(SLOTS, dtype=jnp.int32)[None, :] < counts[:, None]
    key = jnp.where(live, rows, BR).reshape(NB)
    at = jnp.arange(NB, dtype=jnp.int32)
    same = (key[None, :] == key[:, None]) & (at[None, :] < at[:, None])
    rank = jnp.sum(((key[None, :] < key[:, None]) | same).astype(jnp.int32), axis=1)
    more = jnp.sum(same.astype(jnp.int32), axis=1) > 0
    hit = rank[:, None] == at[None, :]
    order = jnp.sum(jnp.where(hit, at[:, None], 0), axis=0)
    cont = jnp.sum((hit & more[:, None]).astype(jnp.int32), axis=0)
    ids = jnp.arange(BR, dtype=jnp.int32)
    upto = jnp.sum((key[None, :] <= ids[:, None]).astype(jnp.int32), axis=1)
    some = jnp.sum((key[None, :] == ids[:, None]).astype(jnp.int32), axis=1) > 0
    last = jnp.where(some, upto - 1, NB)
    return jnp.concatenate([order, cont, key, last])


def body(embeddings, weight, cotangent, adj_blocks, block_rows, block_counts):
    idx = plan(block_rows[0], block_counts[0])
    adj = adj_blocks.reshape(NC, SLOTS * B, B)
    v = pltpu.VMEM
    dma = pltpu.SemaphoreType.DMA
    vmem = pl.BlockSpec(memory_space=pltpu.VMEM)
    tile = (B, F)
    wt = (8, HID)
    return pl.pallas_call(
        kernel,
        out_shape=(
            jax.ShapeDtypeStruct((B, F), BF),
            jax.ShapeDtypeStruct((F, HID), F32),
        ),
        in_specs=[
            pl.BlockSpec(memory_space=pltpu.SMEM), vmem, vmem, vmem, pl.BlockSpec(memory_space=pl.ANY),
        ],
        out_specs=(vmem, vmem),
        scratch_shapes=[
            v((NC, SLOTS * B, B), BF),
            v((NC,) + tile, BF),
            v((NB,) + tile, F32),
            v((NB + 1,) + tile, F32),
            v((NY,) + tile, BF), v((NY,) + tile, BF),
            v((NY,) + tile, BF), v((NY,) + tile, BF),
            v(tile, BF),
            v((BR + 1,) + tile, BF),
            v((16,) + tile, BF), v((16,) + tile, BF),
            v((16,) + tile, F32),
            v((16,) + tile, BF), v((16,) + tile, BF),
            v((NZ,) + tile, BF), v((NZ,) + tile, BF),
            v((BR,) + wt, F32), v((NY,) + wt, F32),
            v((NY,) + wt, F32), v((NY,) + wt, F32),
            v(wt, F32), v(wt, F32),
            v(wt, F32), v((NX,) + wt, F32),
            v(wt, F32), v((NZ,) + wt, F32),
            v((BR,) + wt, F32),
            dma((4,)), dma((31,)), dma((NC,)),
            dma((NY,)), dma((NY,)), dma((NY,)), dma((NY,)),
            dma((15,)), dma((BR,)), dma((16,)), dma((16,)),
            dma((16,)), dma((16,)), dma((NZ,)), dma((NZ,)),
            dma((23,)), dma((23,)),
        ],
        compiler_params=pltpu.CompilerParams(
            collective_id=0, has_side_effects=True, vmem_limit_bytes=48 * 2**20
        ),
    )(idx, embeddings, weight, cotangent, adj)


def solution(mesh):
    return jax.shard_map(
        body,
        mesh=mesh,
        in_specs=(
            P(("col", "row"), None),
            P(),
            P(("row", "col"), None),
            P("row", "col", None, None, None),
            P("row", "col", None),
            P("row", "col"),
        ),
        out_specs=(P(("col", "row"), None), P()),
        check_vma=False,
    )
```

```python
import functools

import jax
import jax.numpy as jnp
from jax import lax
from jax.experimental import pallas as pl
from jax.experimental.pallas import tpu as pltpu
from jax.sharding import PartitionSpec as P

MESH = pl.DeviceIdType.MESH
BR = 16
NX, NZ, NY, NC = 4, 4, 8, 32
SLOTS = 4
VMEM_LIMIT = 40 * 2**20
B = 128
F = 128
HID = 256
NB = NC * SLOTS
BF = jnp.bfloat16
F32 = jnp.float32


def ring4(t):
    return 1 + 2 * t - 3 * (t // 2)


def kernel(
    rows_hbm, counts_hbm, emb_hbm, wgt_hbm, cot_hbm, adj_hbm, gout, gw_out,
    rows_in, counts_in, wide, table, idx, emb, wgt, cot,
    adj, panel, prod, seg, zs, zr, ys, yr, dt, gt, cs, cr, keep, xs, xr, hs, hr,
    lw, lwr, ws, wr, w1, w1r, w2, w2r, w3, w3r, wg,
    sem_a, e_s, e_r, z_s, z_r, y_s, y_r, g_s, g_r, c_s, c_r, x_s, x_r, h_s, h_r,
    w_s, w_r,
):
    row = lax.axis_index("row")
    col = lax.axis_index("col")
    x, zh, core = row // 8, (row // 2) % NZ, row % 2
    zl, y = col // NY, col % NY

    def to_x(d):
        return ((((x + d) % NX) * NZ + zh) * 2 + core, col)

    def to_h(d):
        return ((x * NZ + (zh + d) % NZ) * 2 + core, col)

    def to_y(d):
        return (row, zl * NY + (y + d) % NY)

    sib = ((x * NZ + zh) * 2 + 1 - core, col)
    mate = (row, (1 - zl) * NY + y)

    def node(dx, dz, c):
        return (((x + dx) % NX) * NZ + (zh + dz) % NZ) * 2 + c

    pending = []

    def remote(src, dst, s, r, where):
        return pltpu.make_async_remote_copy(
            src_ref=src, dst_ref=dst, send_sem=s, recv_sem=r, device_id=where, device_id_type=MESH
        )

    def send(cp):
        cp.start()
        pending.append(cp)

    def finish():
        for cp in pending:
            cp.wait_send()

    own_in = pltpu.make_async_copy(emb_hbm, emb, sem_a.at[4])
    own_in.start()
    plan_in = [
        pltpu.make_async_copy(rows_hbm, rows_in, sem_a.at[8]),
        pltpu.make_async_copy(counts_hbm, counts_in, sem_a.at[9]),
    ]
    for cp in plan_in:
        cp.start()
    loads = [
        pltpu.make_async_copy(adj_hbm.at[pl.ds(8 * q, 8)], adj.at[pl.ds(8 * q, 8)], sem_a.at[q])
        for q in range(4)
    ]
    loads.append(pltpu.make_async_copy(wgt_hbm, wgt, sem_a.at[5]))
    loads.append(pltpu.make_async_copy(cot_hbm, cot, sem_a.at[6]))
    for cp in loads:
        cp.start()

    barrier = pltpu.get_barrier_semaphore()
    peers = [sib, mate] + [to_x(d) for d in (1, 2, 3)] + [to_h(d) for d in (1, 2, 3)]
    peers += [to_y(d) for d in range(1, NY)]
    for peer in peers:
        pl.semaphore_signal(barrier, inc=1, device_id=peer, device_id_type=MESH)
    me = node(0, 0, core)
    gt[BR] = jnp.zeros((B, B), BF)
    seg[NB] = jnp.zeros((B, F), F32)
    own_in.wait()
    pl.semaphore_wait(barrier, len(peers))

    def spread(j, n, where, src=None):
        return remote(panel.at[j] if src is None else src, panel.at[j], e_s.at[n], e_r.at[j], where)

    for t, d in enumerate((1, 3, 2)):
        send(spread(me, t, to_h(d), emb))
    for t, d in enumerate((1, 3, 2)):
        send(spread(me, 3 + t, to_x(d), emb))
    send(spread(me, 6, sib, emb))
    panel[me] = emb[...]

    for cp in plan_in:
        cp.wait()
    wide[...] = jnp.zeros((8, B), jnp.int32)
    wide[0:SLOTS, 0:NC] = rows_in[...]
    wide[SLOTS : SLOTS + 1, 0:NC] = counts_in[...]
    lane = lax.broadcasted_iota(jnp.int32, (1, B), 1)
    limit = wide[SLOTS : SLOTS + 1, :]
    key = jnp.zeros((1, B), jnp.int32)
    for q in range(SLOTS):
        mine = jnp.where(limit > q, wide[q : q + 1, :], BR)
        mine = jnp.where(lane < NC, mine, 0)
        key = key + (pltpu.roll(mine, q * NC, 1) if q else mine)
    key_r = jnp.broadcast_to(key, (B, B))
    key_c = key_r.T
    at_r = lax.broadcasted_iota(jnp.int32, (B, B), 1)
    at_c = lax.broadcasted_iota(jnp.int32, (B, B), 0)
    same = jnp.where((key_c == key_r) & (at_c < at_r), 1, 0)
    less = jnp.where(key_c < key_r, 1, 0)
    more = jnp.sum(same, axis=0, keepdims=True)
    rank = more + jnp.sum(less, axis=0, keepdims=True)
    code = rank * 2 + jnp.where(more > 0, 1, 0)
    code_c = jnp.broadcast_to(code, (B, B)).T
    hit = (code_c >> 1) == at_r
    place = (at_c & (NC - 1)) * SLOTS + (at_c >> 5)
    table[0:1, :] = jnp.sum(jnp.where(hit, place, 0), axis=0, keepdims=True)
    table[1:2, :] = jnp.sum(jnp.where(hit, code_c & 1, 0), axis=0, keepdims=True)
    table[2:3, :] = key
    upto = jnp.sum(jnp.where(key_c <= at_r, 1, 0), axis=0, keepdims=True)
    some = jnp.sum(jnp.where(key_c == at_r, 1, 0), axis=0, keepdims=True)
    table[3:4, :] = jnp.where(some > 0, upto - 1, NB)
    table[4:8, :] = jnp.zeros((4, B), jnp.int32)
    to_idx = pltpu.make_async_copy(table, idx, sem_a.at[7])
    to_idx.start()

    def multiply(j):
        prod[pl.ds(j * SLOTS, SLOTS)] = jnp.dot(
            adj[j], panel[j], preferred_element_type=F32
        ).reshape(SLOTS, B, F)

    for cp in loads:
        cp.wait()
    multiply(me)

    def from_z(t, carry):
        j = node(0, ring4(t), core)
        spread(j, 0, sib).wait_recv()
        for q, d in enumerate((1, 3, 2)):
            spread(j, 7 + 4 * t + q, to_x(d)).start()
        spread(j, 7 + 4 * t + 3, sib).start()
        multiply(j)
        return carry

    lax.fori_loop(0, 3, from_z, 0)

    def from_x(t, carry):
        j = node(ring4(t % 3), t // 3, core)
        spread(j, 0, sib).wait_recv()
        spread(j, 19 + t, sib).start()
        multiply(j)
        return carry

    lax.fori_loop(0, 12, from_x, 0)

    def from_sib(t, carry):
        j = node(t % NX, t // NX, 1 - core)
        spread(j, 0, sib).wait_recv()
        multiply(j)
        return carry

    lax.fori_loop(0, 16, from_sib, 0)
    pending += [spread(me, n, sib) for n in range(7, 31)]
    to_idx.wait()

    def segment(i, total):
        total = prod[idx[0, i]] + total * idx[1, i].astype(F32)
        seg[i] = total
        return total

    lax.fori_loop(0, NB, segment, jnp.zeros((B, F), F32))

    order = (4, 3, 5, 2, 6, 1, 7, 0)

    def part(half, d):
        return seg[idx[3, half * NY + (y + d) % NY]]

    def zcopy(d):
        return remote(zs.at[d], zr.at[d], z_s.at[d], z_r.at[d], mate)

    def ycopy(d):
        return remote(ys.at[d], yr.at[d], y_s.at[d], y_r.at[d], to_y(d))

    for d in order:
        zs[d] = part(1 - zl, d).astype(BF)
        send(zcopy(d))
    for d in order[:-1]:
        zcopy(d).wait_recv()
        ys[d] = (part(zl, d) + zr[d].astype(F32)).astype(BF)
        send(ycopy(d))
    zcopy(0).wait_recv()
    total = part(zl, 0) + zr[0].astype(F32)
    for d in (1, 7, 2, 6, 3, 5, 4):
        ycopy(d).wait_recv()
        total = total + yr[d].astype(F32)
    aggregate = total.astype(BF)

    weight = wgt[...]
    pre = jnp.dot(aggregate, weight, preferred_element_type=F32)
    s = 1.0 / (1.0 + jnp.exp(-pre))
    dpre = (cot[...].astype(F32) * (s * (1.0 + pre * (1.0 - s)))).astype(BF)
    dt[...] = lax.dot_general(
        weight, dpre, (((1,), (1,)), ((), ())), preferred_element_type=F32
    ).astype(BF)

    def share(k, n, where, src=None):
        return remote(gt.at[k] if src is None else src, gt.at[k], g_s.at[n], g_r.at[k], where)

    send(share(col, 0, mate, dt))
    for d in (1, 7, 2, 6, 3, 5, 4):
        send(share(col, d, to_y(d), dt))
    gt[col] = dt[...]

    lw[...] = lax.dot_general(
        aggregate, dpre, (((0,), (0,)), ((), ())), preferred_element_type=F32
    ).reshape(BR, 8, HID)
    w_first = remote(lw.at[pl.ds((1 - zl) * NY, NY)], lwr, w_s.at[0], w_r.at[0], mate)
    send(w_first)

    for d in (1, 7, 2, 6, 3, 5, 4):
        k = zl * NY + (y + d) % NY
        share(k, 0, mate).wait_recv()
        send(share(k, 7 + d, mate))

    w_first.wait_recv()

    def w_second(d):
        return remote(ws.at[d], wr.at[d], w_s.at[d], w_r.at[d], to_y(d))

    for d in range(1, NY):
        q = (y + d) % NY
        ws[d] = lw[zl * NY + q] + lwr[q]
        send(w_second(d))
    wtot = lw[zl * NY + y] + lwr[y]

    for d in (0, 1, 7, 2, 6, 3, 5, 4):
        share((1 - zl) * NY + (y + d) % NY, 0, mate).wait_recv()

    w_core = remote(w1, w1r, w_s.at[8], w_r.at[8], sib)

    def w_x(d):
        return remote(w2, w2r.at[x], w_s.at[8 + d], w_r.at[8 + (NX - d) % NX], to_x(d))

    def w_x_recv(d):
        return remote(w2, w2r.at[(x + d) % NX], w_s.at[8 + d], w_r.at[8 + d], to_x(d))

    def w_h(d):
        return remote(w3, w3r.at[zh], w_s.at[11 + d], w_r.at[11 + (NZ - d) % NZ], to_h(d))

    def w_h_recv(d):
        return remote(w3, w3r.at[(zh + d) % NZ], w_s.at[11 + d], w_r.at[11 + d], to_h(d))

    def w_to_core():
        acc = wtot
        for d in range(1, NY):
            w_second(d).wait_recv()
            acc = acc + wr[d]
        w1[...] = acc
        send(w_core)

    def w_to_x():
        w_core.wait_recv()
        first = jnp.where(core == 0, w1[...], w1r[...])
        second = jnp.where(core == 0, w1r[...], w1[...])
        w2[...] = first + second
        w2r[x] = w2[...]
        for d in (1, 3, 2):
            send(w_x(d))

    def w_to_h():
        for d in (1, 3, 2):
            w_x_recv(d).wait_recv()
        w3[...] = (w2r[0] + w2r[1]) + (w2r[2] + w2r[3])
        w3r[zh] = w3[...]
        for d in (1, 3, 2):
            send(w_h(d))

    between = {1: w_to_core, 4: w_to_x, 11: w_to_h}

    def column_grad(j):
        picked = jnp.concatenate([gt[idx[2, q * NC + j]] for q in range(SLOTS)], axis=1)
        return jnp.dot(picked, adj[j], preferred_element_type=F32)

    def ccopy(t):
        return remote(cs.at[t], cr.at[t], c_s.at[t], c_r.at[t], sib)

    def xcopy(t, d):
        return remote(xs.at[t], xr.at[t], x_s.at[t], x_r.at[t], to_x(d))

    def produce(dz, dx):
        t = dz * NX + dx
        cs[t] = column_grad(node(dx, dz, 1 - core)).astype(BF)
        send(ccopy(t))
        keep[t] = column_grad(node(dx, dz, core))

    def pass_on(dz, dx):
        t = dz * NX + dx
        ccopy(t).wait_recv()
        both = keep[t] + cr[t].astype(F32)
        if dx == 0:
            keep[t] = both
        else:
            xs[t] = both.astype(BF)
            send(xcopy(t, dx))

    steps = [(dz, dx) for dz in (2, 1, 3, 0) for dx in (2, 1, 3, 0)]
    lag = 4
    for n in range(len(steps) + lag):
        if n < len(steps):
            produce(*steps[n])
        if n >= lag:
            pass_on(*steps[n - lag])
        if n in between:
            between[n]()

    def hcopy(dz):
        return remote(hs.at[dz], hr.at[dz], h_s.at[dz], h_r.at[dz], to_h(dz))

    def over_x(dz):
        acc = keep[dz * NX]
        for dx in (1, 3, 2):
            xcopy(dz * NX + dx, dx).wait_recv()
            acc = acc + xr[dz * NX + dx].astype(F32)
        return acc

    for dz in (2, 1):
        hs[dz] = over_x(dz).astype(BF)
        send(hcopy(dz))
    hs[3] = over_x(3).astype(BF)
    send(hcopy(3))

    for d in (1, 3, 2):
        w_h_recv(d).wait_recv()
    wg[col] = (w3r[0] + w3r[1]) + (w3r[2] + w3r[3])

    def w_y(d):
        return remote(wg.at[col], wg.at[col], w_s.at[14 + d], w_r.at[14 + (NY - d) % NY], to_y(d))

    def w_y_recv(d):
        k = zl * NY + (y + d) % NY
        return remote(wg.at[k], wg.at[k], w_s.at[14 + d], w_r.at[14 + d], to_y(d))

    for d in order[:-1]:
        send(w_y(d))

    acc = over_x(0)
    for dz in (1, 3, 2):
        hcopy(dz).wait_recv()
        acc = acc + hr[dz].astype(F32)
    gout[...] = acc.T.astype(BF)

    for d in (1, 7, 2, 6, 3, 5, 4):
        w_y_recv(d).wait_recv()
    w_last = remote(
        wg.at[pl.ds(zl * NY, NY)], wg.at[pl.ds(zl * NY, NY)], w_s.at[22], w_r.at[22], mate
    )
    send(w_last)
    w_last.wait_recv()
    gw_out[...] = wg[...].reshape(F, HID)
    finish()


def body(embeddings, weight, cotangent, adj_blocks, block_rows, block_counts):
    adj = adj_blocks.reshape(NC, SLOTS * B, B)
    v = pltpu.VMEM
    dma = pltpu.SemaphoreType.DMA
    vmem = pl.BlockSpec(memory_space=pltpu.VMEM)
    hbm = pl.BlockSpec(memory_space=pltpu.HBM)
    tile = (B, F)
    wt = (8, HID)
    return pl.pallas_call(
        kernel,
        out_shape=(
            jax.ShapeDtypeStruct((B, F), BF),
            jax.ShapeDtypeStruct((F, HID), F32),
        ),
        in_specs=[hbm] * 6,
        out_specs=(vmem, vmem),
        scratch_shapes=[
            v((SLOTS, NC), jnp.int32), v((1, NC), jnp.int32),
            v((8, B), jnp.int32), v((8, B), jnp.int32),
            pltpu.SMEM((8, B), jnp.int32),
            v(tile, BF), v((F, HID), BF), v((B, HID), BF),
            v((NC, SLOTS * B, B), BF),
            v((NC,) + tile, BF),
            v((NB,) + tile, F32),
            v((NB + 1,) + tile, F32),
            v((NY,) + tile, BF), v((NY,) + tile, BF),
            v((NY,) + tile, BF), v((NY,) + tile, BF),
            v(tile, BF),
            v((BR + 1,) + tile, BF),
            v((16,) + tile, BF), v((16,) + tile, BF),
            v((16,) + tile, F32),
            v((16,) + tile, BF), v((16,) + tile, BF),
            v((NZ,) + tile, BF), v((NZ,) + tile, BF),
            v((BR,) + wt, F32), v((NY,) + wt, F32),
            v((NY,) + wt, F32), v((NY,) + wt, F32),
            v(wt, F32), v(wt, F32),
            v(wt, F32), v((NX,) + wt, F32),
            v(wt, F32), v((NZ,) + wt, F32),
            v((BR,) + wt, F32),
            dma((10,)), dma((31,)), dma((NC,)),
            dma((NY,)), dma((NY,)), dma((NY,)), dma((NY,)),
            dma((15,)), dma((BR,)), dma((16,)), dma((16,)),
            dma((16,)), dma((16,)), dma((NZ,)), dma((NZ,)),
            dma((23,)), dma((23,)),
        ],
        compiler_params=pltpu.CompilerParams(
            collective_id=0, has_side_effects=True, vmem_limit_bytes=VMEM_LIMIT
        ),
    )(*[
        pltpu.with_memory_space_constraint(a, pltpu.HBM)
        for a in (block_rows[0].T, block_counts, embeddings, weight, cotangent, adj)
    ])


def solution(mesh):
    return jax.shard_map(
        body,
        mesh=mesh,
        in_specs=(
            P(("col", "row"), None),
            P(),
            P(("row", "col"), None),
            P("row", "col", None, None, None),
            P("row", "col", None),
            P("row", "col"),
        ),
        out_specs=(P(("col", "row"), None), P()),
        check_vma=False,
    )
```

```python
import functools

import jax
import jax.numpy as jnp
from jax import lax
from jax.experimental import pallas as pl
from jax.experimental.pallas import tpu as pltpu
from jax.sharding import PartitionSpec as P

MESH = pl.DeviceIdType.MESH
BR = 16
NX, NZ, NY, NC = 4, 4, 8, 32
SLOTS = 4
VMEM_LIMIT = 40 * 2**20
B = 128
F = 128
HID = 256
NB = NC * SLOTS
BF = jnp.bfloat16
F32 = jnp.float32


def ring4(t):
    return 1 + 2 * t - 3 * lax.div(t, 2)


def wrap(a, n):
    return lax.rem(a, n)


def kernel(
    rows_hbm, counts_hbm, emb_hbm, wgt_hbm, cot_hbm, adj_hbm, gout, gw_out,
    rows_in, counts_in, wide, table, idx, emb, wgt, cot,
    adj, panel, prod, seg, zs, zr, ys, yr, dt, gt, cs, cr, keep, xs, xr, hs, hr,
    lw, lr, ws, wr, pr, wg,
    sem_a, out, e_r, z_r, y_r, g_r, c_r, x_r, h_r, w_r,
):
    row = lax.axis_index("row")
    col = lax.axis_index("col")
    x, zh, core = lax.div(row, 8), wrap(lax.div(row, 2), NZ), wrap(row, 2)
    zl, y = lax.div(col, NY), wrap(col, NY)

    def to_x(d):
        return ((wrap(x + d, NX) * NZ + zh) * 2 + core, col)

    def to_h(d):
        return ((x * NZ + wrap(zh + d, NZ)) * 2 + core, col)

    def to_y(d):
        return (row, zl * NY + wrap(y + d, NY))

    sib = ((x * NZ + zh) * 2 + 1 - core, col)
    mate = (row, (1 - zl) * NY + y)

    def node(dx, dz, c):
        return (wrap(x + dx, NX) * NZ + wrap(zh + dz, NZ)) * 2 + c

    def remote(src, dst, s, r, where):
        return pltpu.make_async_remote_copy(
            src_ref=src, dst_ref=dst, send_sem=s, recv_sem=r, device_id=where, device_id_type=MESH
        )

    def send(cp):
        cp.start()

    def arrived(ref, sem):
        remote(ref, ref, out.at[0], sem, sib).wait_recv()

    def finish():
        groups = (
            panel.at[pl.ds(0, 31)], zs, ys.at[pl.ds(0, 7)], gt.at[pl.ds(0, 15)], cs,
            xs.at[pl.ds(0, 12)], hs.at[pl.ds(0, 3)], lw.at[0], ws.at[pl.ds(0, 15)],
            pr.at[pl.ds(0, 15)], wg.at[0, pl.ds(0, 15)], wg.at[0],
        )
        for n, ref in enumerate(groups):
            remote(ref, ref, out.at[n], out.at[n], sib).wait_send()

    own_in = pltpu.make_async_copy(emb_hbm, emb, sem_a.at[4])
    own_in.start()
    plan_in = [
        pltpu.make_async_copy(rows_hbm, rows_in, sem_a.at[8]),
        pltpu.make_async_copy(counts_hbm, counts_in, sem_a.at[9]),
    ]
    for cp in plan_in:
        cp.start()
    loads = [
        pltpu.make_async_copy(adj_hbm.at[pl.ds(8 * q, 8)], adj.at[pl.ds(8 * q, 8)], sem_a.at[q])
        for q in range(4)
    ]
    loads.append(pltpu.make_async_copy(wgt_hbm, wgt, sem_a.at[5]))
    loads.append(pltpu.make_async_copy(cot_hbm, cot, sem_a.at[6]))
    for cp in loads:
        cp.start()

    barrier = pltpu.get_barrier_semaphore()
    peers = [sib, mate] + [to_x(d) for d in (1, 2, 3)] + [to_h(d) for d in (1, 2, 3)]
    peers += [to_y(d) for d in range(1, NY)]
    for peer in peers:
        pl.semaphore_signal(barrier, inc=1, device_id=peer, device_id_type=MESH)
    me = node(0, 0, core)
    gt[BR] = jnp.zeros((B, B), BF)
    seg[NB] = jnp.zeros((B, F), F32)
    own_in.wait()
    pl.semaphore_wait(barrier, len(peers))

    def spread(j, where, src=None, sem=None):
        return remote(
            panel.at[j] if src is None else src, panel.at[j], out.at[0],
            e_r.at[j] if sem is None else sem, where,
        )

    for d in (1, 3, 2):
        send(spread(me, to_h(d), emb))
    for d in (1, 3, 2):
        send(spread(me, to_x(d), emb))
    send(spread(me, sib, emb, e_r.at[NC]))
    panel[me] = emb[...]

    for cp in plan_in:
        cp.wait()
    wide[...] = jnp.zeros((8, B), jnp.int32)
    wide[0:SLOTS, 0:NC] = rows_in[...]
    wide[SLOTS : SLOTS + 1, 0:NC] = counts_in[...]
    lane = lax.broadcasted_iota(jnp.int32, (1, B), 1)
    limit = wide[SLOTS : SLOTS + 1, :]
    key = jnp.zeros((1, B), jnp.int32)
    for q in range(SLOTS):
        mine = jnp.where(limit > q, wide[q : q + 1, :], BR)
        mine = jnp.where(lane < NC, mine, 0)
        key = key + (pltpu.roll(mine, q * NC, 1) if q else mine)
    key_r = jnp.broadcast_to(key, (B, B))
    key_c = key_r.T
    at_r = lax.broadcasted_iota(jnp.int32, (B, B), 1)
    at_c = lax.broadcasted_iota(jnp.int32, (B, B), 0)
    same = jnp.where((key_c == key_r) & (at_c < at_r), 1, 0)
    less = jnp.where(key_c < key_r, 1, 0)
    more = jnp.sum(same, axis=0, keepdims=True)
    rank = more + jnp.sum(less, axis=0, keepdims=True)
    code = rank * 2 + jnp.where(more > 0, 1, 0)
    code_c = jnp.broadcast_to(code, (B, B)).T
    hit = (code_c >> 1) == at_r
    place = (at_c & (NC - 1)) * SLOTS + (at_c >> 5)
    table[0:1, :] = jnp.sum(jnp.where(hit, place, 0), axis=0, keepdims=True)
    table[1:2, :] = jnp.sum(jnp.where(hit, code_c & 1, 0), axis=0, keepdims=True)
    table[2:3, :] = key
    upto = jnp.sum(jnp.where(key_c <= at_r, 1, 0), axis=0, keepdims=True)
    some = jnp.sum(jnp.where(key_c == at_r, 1, 0), axis=0, keepdims=True)
    table[3:4, :] = jnp.where(some > 0, upto - 1, NB)
    table[4:8, :] = jnp.zeros((4, B), jnp.int32)
    to_idx = pltpu.make_async_copy(table, idx, sem_a.at[7])
    to_idx.start()

    def multiply(j):
        prod[pl.ds(j * SLOTS, SLOTS)] = jnp.dot(
            adj[j], panel[j], preferred_element_type=F32
        ).reshape(SLOTS, B, F)

    for cp in loads:
        cp.wait()
    multiply(me)

    for dz in (1, 3, 2):
        j = node(0, dz, core)
        spread(j, sib).wait_recv()
        for d in (1, 3, 2):
            send(spread(j, to_x(d)))
        send(spread(j, sib, None, e_r.at[NC + dz]))
        multiply(j)

    def from_x(dz, t, carry):
        j = node(ring4(t), dz, core)
        spread(j, sib).wait_recv()
        send(spread(j, sib, None, e_r.at[NC + dz]))
        multiply(j)
        return carry

    def from_sib(dz, t, carry):
        multiply(node(t, dz, 1 - core))
        return carry

    for dz in (0, 1, 3, 2):
        lax.fori_loop(0, 3, functools.partial(from_x, dz), 0)
    for dz in (0, 1, 3, 2):
        arrived(panel.at[pl.ds(0, NX)], e_r.at[NC + dz])
        lax.fori_loop(0, NX, functools.partial(from_sib, dz), 0)
    to_idx.wait()

    def segment(i, total):
        total = prod[idx[0, i]] + total * idx[1, i].astype(F32)
        seg[i] = total
        return total

    lax.fori_loop(0, NB, segment, jnp.zeros((B, F), F32))

    order = (4, 3, 5, 2, 6, 1, 7, 0)

    def part(half, d):
        return seg[idx[3, half * NY + wrap(y + d, NY)]]

    def zcopy(d):
        return remote(zs.at[d], zr.at[d], out.at[1], z_r.at[d], mate)

    def ycopy(d):
        return remote(ys.at[d], yr.at[d], out.at[2], y_r.at[0], to_y(d))

    for d in order:
        zs[d] = part(1 - zl, d).astype(BF)
        send(zcopy(d))
    for d in order[:-1]:
        zcopy(d).wait_recv()
        ys[d] = (part(zl, d) + zr[d].astype(F32)).astype(BF)
        send(ycopy(d))
    zcopy(0).wait_recv()
    total = part(zl, 0) + zr[0].astype(F32)
    arrived(yr.at[pl.ds(1, NY - 1)], y_r.at[0])
    for d in range(1, NY):
        total = total + yr[d].astype(F32)
    aggregate = total.astype(BF)

    weight = wgt[...]
    pre = jnp.dot(aggregate, weight, preferred_element_type=F32)
    s = 1.0 / (1.0 + jnp.exp(-pre))
    dpre = (cot[...].astype(F32) * (s * (1.0 + pre * (1.0 - s)))).astype(BF)
    dt[...] = lax.dot_general(
        weight, dpre, (((1,), (1,)), ((), ())), preferred_element_type=F32
    ).astype(BF)

    def share(k, where, src=None, sem=None):
        return remote(
            gt.at[k] if src is None else src, gt.at[k], out.at[3],
            g_r.at[k] if sem is None else sem, where,
        )

    send(share(col, mate, dt, g_r.at[BR]))
    for d in (1, 7, 2, 6, 3, 5, 4):
        send(share(col, to_y(d), dt))
    gt[col] = dt[...]

    grad_w = lax.dot_general(
        aggregate, dpre, (((0,), (0,)), ((), ())), preferred_element_type=F32
    )
    for c in range(2):
        lw[c] = grad_w[:, c * 128 : (c + 1) * 128].reshape(BR, 8, 128)
    chip = lax.div(row, 2)

    def w_half():
        return remote(lw.at[1 - core], lr, out.at[7], w_r.at[0], sib)

    def w_to_col():
        arrived(lr, w_r.at[0])
        ws[...] = lw[core] + lr[...]
        for d in range(1, BR):
            k = wrap(col + d, BR)
            send(remote(ws.at[k], wr.at[col], out.at[8], w_r.at[1], (row, k)))
        wr[col] = ws[col]

    def w_to_plane():
        arrived(wr.at[pl.ds(0, 15)], w_r.at[1])
        pr[chip] = jnp.sum(wr[...], axis=0)
        for d in range(1, 16):
            q = wrap(chip + d, 16)
            send(remote(pr.at[chip], pr.at[chip], out.at[9], w_r.at[2], (q * 2 + core, col)))

    def w_from_plane():
        arrived(pr.at[pl.ds(0, 15)], w_r.at[2])
        wg[core, col] = jnp.sum(pr[...], axis=0)
        for d in range(1, BR):
            k = wrap(col + d, BR)
            send(remote(wg.at[core, col], wg.at[core, col], out.at[10], w_r.at[3], (row, k)))

    def w_last():
        return remote(wg.at[core], wg.at[core], out.at[11], w_r.at[4], sib)

    def w_to_sib():
        arrived(wg.at[core, pl.ds(0, 15)], w_r.at[3])
        send(w_last())

    send(w_half())
    for n, d in enumerate((1, 7, 2, 6, 3, 5, 4)):
        k = zl * NY + wrap(y + d, NY)
        share(k, mate).wait_recv()
        send(share(k, mate, None, g_r.at[BR]))
        if n == 1:
            w_to_col()

    arrived(gt.at[pl.ds(0, NY)], g_r.at[BR])
    w_to_plane()
    def column_grad(j):
        picked = jnp.concatenate([gt[idx[2, q * NC + j]] for q in range(SLOTS)], axis=1)
        return jnp.dot(picked, adj[j], preferred_element_type=F32)

    def ccopy(t):
        return remote(cs.at[t], cr.at[t], out.at[4], c_r.at[t], sib)

    def xcopy(t, d):
        return remote(xs.at[t], xr.at[t], out.at[5], x_r.at[t // NX], to_x(d))

    def produce(dz, dx):
        t = dz * NX + dx
        cs[t] = column_grad(node(dx, dz, 1 - core)).astype(BF)
        send(ccopy(t))
        keep[t] = column_grad(node(dx, dz, core))

    def pass_on(dz, dx):
        t = dz * NX + dx
        ccopy(t).wait_recv()
        both = keep[t] + cr[t].astype(F32)
        if dx == 0:
            keep[t] = both
        else:
            xs[t] = both.astype(BF)
            send(xcopy(t, dx))

    steps = [(dz, dx) for dz in (2, 1, 3, 0) for dx in (2, 1, 3, 0)]
    lag = 4
    for n in range(len(steps) + lag):
        if n < len(steps):
            produce(*steps[n])
        if n >= lag:
            pass_on(*steps[n - lag])
        if n == 10:
            w_from_plane()

    def hcopy(dz):
        return remote(hs.at[dz], hr.at[dz], out.at[6], h_r.at[0], to_h(dz))

    def over_x(dz):
        acc = keep[dz * NX]
        arrived(xr.at[pl.ds(dz * NX + 1, NX - 1)], x_r.at[dz])
        for dx in (1, 2, 3):
            acc = acc + xr[dz * NX + dx].astype(F32)
        return acc

    for dz in (2, 1):
        hs[dz] = over_x(dz).astype(BF)
        send(hcopy(dz))
    hs[3] = over_x(3).astype(BF)
    send(hcopy(3))

    w_to_sib()
    acc = over_x(0)
    arrived(hr.at[pl.ds(1, NZ - 1)], h_r.at[0])
    for dz in (1, 2, 3):
        acc = acc + hr[dz].astype(F32)
    gout[...] = acc.T.astype(BF)

    w_last().wait_recv()
    for c in range(2):
        gw_out[:, c * 128 : (c + 1) * 128] = wg[c].reshape(F, 128)
    finish()


def body(embeddings, weight, cotangent, adj_blocks, block_rows, block_counts):
    adj = adj_blocks.reshape(NC, SLOTS * B, B)
    v = pltpu.VMEM
    dma = pltpu.SemaphoreType.DMA
    vmem = pl.BlockSpec(memory_space=pltpu.VMEM)
    hbm = pl.BlockSpec(memory_space=pltpu.HBM)
    tile = (B, F)
    wt = (8, 128)
    return pl.pallas_call(
        kernel,
        out_shape=(
            jax.ShapeDtypeStruct((B, F), BF),
            jax.ShapeDtypeStruct((F, HID), F32),
        ),
        in_specs=[hbm] * 6,
        out_specs=(vmem, vmem),
        scratch_shapes=[
            v((SLOTS, NC), jnp.int32), v((1, NC), jnp.int32),
            v((8, B), jnp.int32), v((8, B), jnp.int32),
            pltpu.SMEM((8, B), jnp.int32),
            v(tile, BF), v((F, HID), BF), v((B, HID), BF),
            v((NC, SLOTS * B, B), BF),
            v((NC,) + tile, BF),
            v((NB,) + tile, F32),
            v((NB + 1,) + tile, F32),
            v((NY,) + tile, BF), v((NY,) + tile, BF),
            v((NY,) + tile, BF), v((NY,) + tile, BF),
            v(tile, BF),
            v((BR + 1,) + tile, BF),
            v((16,) + tile, BF), v((16,) + tile, BF),
            v((16,) + tile, F32),
            v((16,) + tile, BF), v((16,) + tile, BF),
            v((NZ,) + tile, BF), v((NZ,) + tile, BF),
            v((2, BR) + wt, F32), v((BR,) + wt, F32),
            v((BR,) + wt, F32), v((BR,) + wt, F32),
            v((16,) + wt, F32), v((2, BR) + wt, F32),
            dma((10,)), dma((12,)), dma((NC + NZ,)), dma((NY,)), dma((1,)), dma((BR + 1,)),
            dma((16,)), dma((NZ,)), dma((1,)), dma((5,)),
        ],
        compiler_params=pltpu.CompilerParams(
            collective_id=0, has_side_effects=True, vmem_limit_bytes=VMEM_LIMIT
        ),
    )(*[
        pltpu.with_memory_space_constraint(a, pltpu.HBM)
        for a in (block_rows[0].T, block_counts, embeddings, weight, cotangent, adj)
    ])


def solution(mesh):
    return jax.shard_map(
        body,
        mesh=mesh,
        in_specs=(
            P(("col", "row"), None),
            P(),
            P(("row", "col"), None),
            P("row", "col", None, None, None),
            P("row", "col", None),
            P("row", "col"),
        ),
        out_specs=(P(("col", "row"), None), P()),
        check_vma=False,
    )
```

```python
import functools

import jax
import jax.numpy as jnp
from jax import lax
from jax.experimental import pallas as pl
from jax.experimental.pallas import tpu as pltpu
from jax.sharding import PartitionSpec as P

MESH = pl.DeviceIdType.MESH
BR = 16
NX, NZ, NY, NC = 4, 4, 8, 32
SLOTS = 4
VMEM_LIMIT = 40 * 2**20
B = 128
F = 128
HID = 256
NB = NC * SLOTS
BF = jnp.bfloat16
F32 = jnp.float32


def ring4(t):
    return 1 + 2 * t - 3 * lax.div(t, 2)


def wrap(a, n):
    return lax.rem(a, n)


def kernel(
    rows_hbm, counts_hbm, emb_hbm, wgt_hbm, cot_hbm, adj_hbm, gout, gw_out,
    rows_in, counts_in, wide, table, idx, emb, wgt, cot,
    adj, panel, prod, seg, zs, zr, ys, yr, dt, gt, cs, cr, keep, xs, xr, hs, hr,
    lw, lr, ws, wr, pr, wg,
    sem_a, out, e_r, z_r, y_r, g_r, c_r, x_r, h_r, w_r,
):
    row = lax.axis_index("row")
    col = lax.axis_index("col")
    x, zh, core = lax.div(row, 8), wrap(lax.div(row, 2), NZ), wrap(row, 2)
    zl, y = lax.div(col, NY), wrap(col, NY)

    def to_x(d):
        return ((wrap(x + d, NX) * NZ + zh) * 2 + core, col)

    def to_h(d):
        return ((x * NZ + wrap(zh + d, NZ)) * 2 + core, col)

    def to_y(d):
        return (row, zl * NY + wrap(y + d, NY))

    sib = ((x * NZ + zh) * 2 + 1 - core, col)
    mate = (row, (1 - zl) * NY + y)

    def node(dx, dz, c):
        return (wrap(x + dx, NX) * NZ + wrap(zh + dz, NZ)) * 2 + c

    def remote(src, dst, s, r, where):
        return pltpu.make_async_remote_copy(
            src_ref=src, dst_ref=dst, send_sem=s, recv_sem=r, device_id=where, device_id_type=MESH
        )

    def send(cp):
        cp.start()

    def arrived(ref, sem):
        remote(ref, ref, out.at[0], sem, sib).wait_recv()

    def finish():
        groups = (
            panel.at[pl.ds(0, 31)], zs, ys.at[pl.ds(0, 7)], gt.at[pl.ds(0, 15)], cs,
            xs.at[pl.ds(0, 12)], hs.at[pl.ds(0, 3)], lw.at[0], ws.at[pl.ds(0, 15)],
            pr.at[pl.ds(0, 15)], wg.at[0, pl.ds(0, 15)], wg.at[0],
        )
        for n, ref in enumerate(groups):
            remote(ref, ref, out.at[n], out.at[n], sib).wait_send()

    own_in = pltpu.make_async_copy(emb_hbm, emb, sem_a.at[4])
    own_in.start()
    barrier = pltpu.get_barrier_semaphore()
    peers = [sib, mate] + [to_x(d) for d in (1, 2, 3)] + [to_h(d) for d in (1, 2, 3)]
    peers += [to_y(d) for d in range(1, NY)]
    for peer in peers:
        pl.semaphore_signal(barrier, inc=1, device_id=peer, device_id_type=MESH)
    plan_in = [
        pltpu.make_async_copy(rows_hbm, rows_in, sem_a.at[8]),
        pltpu.make_async_copy(counts_hbm, counts_in, sem_a.at[9]),
    ]
    for cp in plan_in:
        cp.start()
    loads = [
        pltpu.make_async_copy(adj_hbm.at[pl.ds(8 * q, 8)], adj.at[pl.ds(8 * q, 8)], sem_a.at[q])
        for q in range(4)
    ]
    loads.append(pltpu.make_async_copy(wgt_hbm, wgt, sem_a.at[5]))
    loads.append(pltpu.make_async_copy(cot_hbm, cot, sem_a.at[6]))
    for cp in loads:
        cp.start()

    me = node(0, 0, core)
    gt[BR] = jnp.zeros((B, B), BF)
    seg[NB] = jnp.zeros((B, F), F32)
    own_in.wait()
    pl.semaphore_wait(barrier, len(peers))

    def spread(j, where, src=None, sem=None):
        return remote(
            panel.at[j] if src is None else src, panel.at[j], out.at[0],
            e_r.at[j] if sem is None else sem, where,
        )

    for d in (1, 3, 2):
        send(spread(me, to_h(d), emb))
    for d in (1, 3, 2):
        send(spread(me, to_x(d), emb))
    send(spread(me, sib, emb, e_r.at[NC]))
    panel[me] = emb[...]

    for cp in plan_in:
        cp.wait()
    wide[...] = jnp.zeros((8, B), jnp.int32)
    wide[0:SLOTS, 0:NC] = rows_in[...]
    wide[SLOTS : SLOTS + 1, 0:NC] = counts_in[...]
    lane = lax.broadcasted_iota(jnp.int32, (1, B), 1)
    limit = wide[SLOTS : SLOTS + 1, :]
    key = jnp.zeros((1, B), jnp.int32)
    for q in range(SLOTS):
        mine = jnp.where(limit > q, wide[q : q + 1, :], BR)
        mine = jnp.where(lane < NC, mine, 0)
        key = key + (pltpu.roll(mine, q * NC, 1) if q else mine)
    key_r = jnp.broadcast_to(key, (B, B))
    key_c = key_r.T
    at_r = lax.broadcasted_iota(jnp.int32, (B, B), 1)
    at_c = lax.broadcasted_iota(jnp.int32, (B, B), 0)
    same = jnp.where((key_c == key_r) & (at_c < at_r), 1, 0)
    less = jnp.where(key_c < key_r, 1, 0)
    more = jnp.sum(same, axis=0, keepdims=True)
    rank = more + jnp.sum(less, axis=0, keepdims=True)
    code = rank * 2 + jnp.where(more > 0, 1, 0)
    code_c = jnp.broadcast_to(code, (B, B)).T
    hit = (code_c >> 1) == at_r
    place = (at_c & (NC - 1)) * SLOTS + (at_c >> 5)
    table[0:1, :] = jnp.sum(jnp.where(hit, place, 0), axis=0, keepdims=True)
    table[1:2, :] = jnp.sum(jnp.where(hit, code_c & 1, 0), axis=0, keepdims=True)
    table[2:3, :] = key
    upto = jnp.sum(jnp.where(key_c <= at_r, 1, 0), axis=0, keepdims=True)
    some = jnp.sum(jnp.where(key_c == at_r, 1, 0), axis=0, keepdims=True)
    table[3:4, :] = jnp.where(some > 0, upto - 1, NB)
    table[4:8, :] = jnp.zeros((4, B), jnp.int32)
    to_idx = pltpu.make_async_copy(table, idx, sem_a.at[7])
    to_idx.start()

    def multiply(j):
        prod[pl.ds(j * SLOTS, SLOTS)] = jnp.dot(
            adj[j], panel[j], preferred_element_type=F32
        ).reshape(SLOTS, B, F)

    for cp in loads:
        cp.wait()
    multiply(me)

    for dz in (1, 3, 2):
        j = node(0, dz, core)
        spread(j, sib).wait_recv()
        for d in (1, 3, 2):
            send(spread(j, to_x(d)))
        send(spread(j, sib, None, e_r.at[NC + dz]))
        multiply(j)

    def from_x(dz, t, carry):
        j = node(ring4(t), dz, core)
        spread(j, sib).wait_recv()
        send(spread(j, sib, None, e_r.at[NC + dz]))
        multiply(j)
        return carry

    def from_sib(dz, t, carry):
        multiply(node(t, dz, 1 - core))
        return carry

    for dz in (0, 1, 3, 2):
        lax.fori_loop(0, 3, functools.partial(from_x, dz), 0)
    for dz in (0, 1, 3, 2):
        arrived(panel.at[pl.ds(0, NX)], e_r.at[NC + dz])
        lax.fori_loop(0, NX, functools.partial(from_sib, dz), 0)
    to_idx.wait()

    def segment(i, total):
        total = prod[idx[0, i]] + total * idx[1, i].astype(F32)
        seg[i] = total
        return total

    lax.fori_loop(0, NB, segment, jnp.zeros((B, F), F32))

    order = (4, 3, 5, 2, 6, 1, 7, 0)

    def part(half, d):
        return seg[idx[3, half * NY + wrap(y + d, NY)]]

    def zcopy(d):
        return remote(zs.at[d], zr.at[d], out.at[1], z_r.at[d], mate)

    def ycopy(d):
        return remote(ys.at[d], yr.at[d], out.at[2], y_r.at[0], to_y(d))

    for d in order:
        zs[d] = part(1 - zl, d).astype(BF)
        send(zcopy(d))
    for d in order[:-1]:
        zcopy(d).wait_recv()
        ys[d] = (part(zl, d) + zr[d].astype(F32)).astype(BF)
        send(ycopy(d))
    zcopy(0).wait_recv()
    total = part(zl, 0) + zr[0].astype(F32)
    arrived(yr.at[pl.ds(1, NY - 1)], y_r.at[0])
    for d in range(1, NY):
        total = total + yr[d].astype(F32)
    aggregate = total.astype(BF)

    weight = wgt[...]
    pre = jnp.dot(aggregate, weight, preferred_element_type=F32)
    s = 1.0 / (1.0 + jnp.exp(-pre))
    dpre = (cot[...].astype(F32) * (s * (1.0 + pre * (1.0 - s)))).astype(BF)
    dt[...] = lax.dot_general(
        weight, dpre, (((1,), (1,)), ((), ())), preferred_element_type=F32
    ).astype(BF)

    def share(k, where, src=None, sem=None):
        return remote(
            gt.at[k] if src is None else src, gt.at[k], out.at[3],
            g_r.at[k] if sem is None else sem, where,
        )

    send(share(col, mate, dt, g_r.at[BR]))
    for d in (1, 7, 2, 6, 3, 5, 4):
        send(share(col, to_y(d), dt))
    gt[col] = dt[...]

    grad_w = lax.dot_general(
        aggregate, dpre, (((0,), (0,)), ((), ())), preferred_element_type=F32
    )
    for c in range(2):
        lw[c] = grad_w[:, c * 128 : (c + 1) * 128].reshape(BR, 8, 128)
    chip = lax.div(row, 2)

    def w_half():
        return remote(lw.at[1 - core], lr, out.at[7], w_r.at[0], sib)

    def w_to_col():
        arrived(lr, w_r.at[0])
        ws[...] = lw[core] + lr[...]
        for d in range(1, BR):
            k = wrap(col + d, BR)
            send(remote(ws.at[k], wr.at[col], out.at[8], w_r.at[1], (row, k)))
        wr[col] = ws[col]

    def w_to_plane():
        arrived(wr.at[pl.ds(0, 15)], w_r.at[1])
        pr[chip] = jnp.sum(wr[...], axis=0)
        for d in range(1, 16):
            q = wrap(chip + d, 16)
            send(remote(pr.at[chip], pr.at[chip], out.at[9], w_r.at[2], (q * 2 + core, col)))

    def w_from_plane():
        arrived(pr.at[pl.ds(0, 15)], w_r.at[2])
        wg[core, col] = jnp.sum(pr[...], axis=0)
        for d in range(1, BR):
            k = wrap(col + d, BR)
            send(remote(wg.at[core, col], wg.at[core, col], out.at[10], w_r.at[3], (row, k)))

    def w_last():
        return remote(wg.at[core], wg.at[core], out.at[11], w_r.at[4], sib)

    def w_to_sib():
        arrived(wg.at[core, pl.ds(0, 15)], w_r.at[3])
        send(w_last())

    send(w_half())
    for n, d in enumerate((1, 7, 2, 6, 3, 5, 4)):
        k = zl * NY + wrap(y + d, NY)
        share(k, mate).wait_recv()
        send(share(k, mate, None, g_r.at[BR]))
        if n == 1:
            w_to_col()

    arrived(gt.at[pl.ds(0, NY)], g_r.at[BR])
    def column_grad(j):
        picked = jnp.concatenate([gt[idx[2, q * NC + j]] for q in range(SLOTS)], axis=1)
        return jnp.dot(picked, adj[j], preferred_element_type=F32)

    def ccopy(t):
        return remote(cs.at[t], cr.at[t], out.at[4], c_r.at[t], sib)

    def xcopy(t, d):
        return remote(xs.at[t], xr.at[t], out.at[5], x_r.at[t // NX], to_x(d))

    def produce(dz, dx):
        t = dz * NX + dx
        cs[t] = column_grad(node(dx, dz, 1 - core)).astype(BF)
        send(ccopy(t))
        keep[t] = column_grad(node(dx, dz, core))

    def pass_on(dz, dx):
        t = dz * NX + dx
        ccopy(t).wait_recv()
        both = keep[t] + cr[t].astype(F32)
        if dx == 0:
            keep[t] = both
        else:
            xs[t] = both.astype(BF)
            send(xcopy(t, dx))

    steps = [(dz, dx) for dz in (2, 1, 3, 0) for dx in (2, 1, 3, 0)]
    lag = 4
    for n in range(len(steps) + lag):
        if n < len(steps):
            produce(*steps[n])
        if n >= lag:
            pass_on(*steps[n - lag])
        if n == 3:
            w_to_plane()
        if n == 15:
            w_from_plane()

    def hcopy(dz):
        return remote(hs.at[dz], hr.at[dz], out.at[6], h_r.at[0], to_h(dz))

    def over_x(dz):
        acc = keep[dz * NX]
        arrived(xr.at[pl.ds(dz * NX + 1, NX - 1)], x_r.at[dz])
        for dx in (1, 2, 3):
            acc = acc + xr[dz * NX + dx].astype(F32)
        return acc

    for dz in (2, 1):
        hs[dz] = over_x(dz).astype(BF)
        send(hcopy(dz))
    hs[3] = over_x(3).astype(BF)
    send(hcopy(3))

    w_to_sib()
    acc = over_x(0)
    arrived(hr.at[pl.ds(1, NZ - 1)], h_r.at[0])
    for dz in (1, 2, 3):
        acc = acc + hr[dz].astype(F32)
    gout[...] = acc.T.astype(BF)

    w_last().wait_recv()
    for c in range(2):
        gw_out[:, c * 128 : (c + 1) * 128] = wg[c].reshape(F, 128)
    finish()


def body(embeddings, weight, cotangent, adj_blocks, block_rows, block_counts):
    adj = adj_blocks.reshape(NC, SLOTS * B, B)
    v = pltpu.VMEM
    dma = pltpu.SemaphoreType.DMA
    vmem = pl.BlockSpec(memory_space=pltpu.VMEM)
    hbm = pl.BlockSpec(memory_space=pltpu.HBM)
    tile = (B, F)
    wt = (8, 128)
    return pl.pallas_call(
        kernel,
        out_shape=(
            jax.ShapeDtypeStruct((B, F), BF),
            jax.ShapeDtypeStruct((F, HID), F32),
        ),
        in_specs=[hbm] * 6,
        out_specs=(vmem, vmem),
        scratch_shapes=[
            v((SLOTS, NC), jnp.int32), v((1, NC), jnp.int32),
            v((8, B), jnp.int32), v((8, B), jnp.int32),
            pltpu.SMEM((8, B), jnp.int32),
            v(tile, BF), v((F, HID), BF), v((B, HID), BF),
            v((NC, SLOTS * B, B), BF),
            v((NC,) + tile, BF),
            v((NB,) + tile, F32),
            v((NB + 1,) + tile, F32),
            v((NY,) + tile, BF), v((NY,) + tile, BF),
            v((NY,) + tile, BF), v((NY,) + tile, BF),
            v(tile, BF),
            v((BR + 1,) + tile, BF),
            v((16,) + tile, BF), v((16,) + tile, BF),
            v((16,) + tile, F32),
            v((16,) + tile, BF), v((16,) + tile, BF),
            v((NZ,) + tile, BF), v((NZ,) + tile, BF),
            v((2, BR) + wt, F32), v((BR,) + wt, F32),
            v((BR,) + wt, F32), v((BR,) + wt, F32),
            v((16,) + wt, F32), v((2, BR) + wt, F32),
            dma((10,)), dma((12,)), dma((NC + NZ,)), dma((NY,)), dma((1,)), dma((BR + 1,)),
            dma((16,)), dma((NZ,)), dma((1,)), dma((5,)),
        ],
        compiler_params=pltpu.CompilerParams(
            collective_id=0, has_side_effects=True, vmem_limit_bytes=VMEM_LIMIT
        ),
    )(*[
        pltpu.with_memory_space_constraint(a, pltpu.HBM)
        for a in (block_rows[0].T, block_counts, embeddings, weight, cotangent, adj)
    ])


def solution(mesh):
    return jax.shard_map(
        body,
        mesh=mesh,
        in_specs=(
            P(("col", "row"), None),
            P(),
            P(("row", "col"), None),
            P("row", "col", None, None, None),
            P("row", "col", None),
            P("row", "col"),
        ),
        out_specs=(P(("col", "row"), None), P()),
        check_vma=False,
    )
```

```python
import functools

import jax
import jax.numpy as jnp
from jax import lax
from jax.experimental import pallas as pl
from jax.experimental.pallas import tpu as pltpu
from jax.sharding import PartitionSpec as P

MESH = pl.DeviceIdType.MESH
BR = 16
NX, NZ, NY, NC = 4, 4, 8, 32
SLOTS = 4
VMEM_LIMIT = 40 * 2**20
B = 128
F = 128
HID = 256
NB = NC * SLOTS
BF = jnp.bfloat16
F32 = jnp.float32


def ring4(t):
    return 1 + 2 * t - 3 * lax.div(t, 2)


def wrap(a, n):
    return lax.rem(a, n)


def kernel(
    rows_hbm, counts_hbm, emb_hbm, wgt_hbm, cot_hbm, adj_hbm, gout, gw_out,
    rows_in, counts_in, wide, table, idx, emb, wgt, cot,
    adj, panel, prod, seg, zs, zr, ys, yr, dt, gt, cs, cr, keep, xs, xr, hs, hr,
    lw, lr, ws, wr, pr, wg,
    sem_a, out, e_r, z_r, y_r, g_r, c_r, x_r, h_r, w_r,
):
    row = lax.axis_index("row")
    col = lax.axis_index("col")
    x, zh, core = lax.div(row, 8), wrap(lax.div(row, 2), NZ), wrap(row, 2)
    zl, y = lax.div(col, NY), wrap(col, NY)

    def to_x(d):
        return ((wrap(x + d, NX) * NZ + zh) * 2 + core, col)

    def to_h(d):
        return ((x * NZ + wrap(zh + d, NZ)) * 2 + core, col)

    def to_y(d):
        return (row, zl * NY + wrap(y + d, NY))

    sib = ((x * NZ + zh) * 2 + 1 - core, col)
    mate = (row, (1 - zl) * NY + y)

    def node(dx, dz, c):
        return (wrap(x + dx, NX) * NZ + wrap(zh + dz, NZ)) * 2 + c

    def remote(src, dst, s, r, where):
        return pltpu.make_async_remote_copy(
            src_ref=src, dst_ref=dst, send_sem=s, recv_sem=r, device_id=where, device_id_type=MESH
        )

    def send(cp):
        cp.start()

    def arrived(ref, sem):
        remote(ref, ref, out.at[0], sem, sib).wait_recv()

    def finish():
        groups = (
            panel.at[pl.ds(0, 31)], zs, ys.at[pl.ds(0, 7)], gt.at[pl.ds(0, 15)], cs,
            xs.at[pl.ds(0, 12)], hs.at[pl.ds(0, 3)], lw.at[0], ws.at[pl.ds(0, 15)],
            pr.at[pl.ds(0, 15)], wg.at[0, pl.ds(0, 15)], wg.at[0],
        )
        for n, ref in enumerate(groups):
            remote(ref, ref, out.at[n], out.at[n], sib).wait_send()

    own_in = pltpu.make_async_copy(emb_hbm, emb, sem_a.at[4])
    own_in.start()
    barrier = pltpu.get_barrier_semaphore()
    peers = [sib, mate] + [to_x(d) for d in (1, 2, 3)] + [to_h(d) for d in (1, 2, 3)]
    peers += [to_y(d) for d in range(1, NY)]
    for peer in peers:
        pl.semaphore_signal(barrier, inc=1, device_id=peer, device_id_type=MESH)
    plan_in = [
        pltpu.make_async_copy(rows_hbm, rows_in, sem_a.at[8]),
        pltpu.make_async_copy(counts_hbm, counts_in, sem_a.at[9]),
    ]
    for cp in plan_in:
        cp.start()
    loads = [
        pltpu.make_async_copy(adj_hbm.at[pl.ds(8 * q, 8)], adj.at[pl.ds(8 * q, 8)], sem_a.at[q])
        for q in range(4)
    ]
    loads.append(pltpu.make_async_copy(wgt_hbm, wgt, sem_a.at[5]))
    loads.append(pltpu.make_async_copy(cot_hbm, cot, sem_a.at[6]))
    for cp in loads:
        cp.start()

    me = node(0, 0, core)
    gt[BR] = jnp.zeros((B, B), BF)
    seg[NB] = jnp.zeros((B, F), F32)
    own_in.wait()
    pl.semaphore_wait(barrier, len(peers))

    def spread(j, where, src=None, sem=None):
        return remote(
            panel.at[j] if src is None else src, panel.at[j], out.at[0],
            e_r.at[j] if sem is None else sem, where,
        )

    for d in (1, 3, 2):
        send(spread(me, to_h(d), emb))
    for d in (1, 3, 2):
        send(spread(me, to_x(d), emb))
    send(spread(me, sib, emb, e_r.at[NC]))
    panel[me] = emb[...]

    for cp in plan_in:
        cp.wait()
    wide[...] = jnp.zeros((8, B), jnp.int32)
    wide[0:SLOTS, 0:NC] = rows_in[...]
    wide[SLOTS : SLOTS + 1, 0:NC] = counts_in[...]
    lane = lax.broadcasted_iota(jnp.int32, (1, B), 1)
    limit = wide[SLOTS : SLOTS + 1, :]
    key = jnp.zeros((1, B), jnp.int32)
    for q in range(SLOTS):
        mine = jnp.where(limit > q, wide[q : q + 1, :], BR)
        mine = jnp.where(lane < NC, mine, 0)
        key = key + (pltpu.roll(mine, q * NC, 1) if q else mine)
    key_r = jnp.broadcast_to(key, (B, B))
    key_c = key_r.T
    at_r = lax.broadcasted_iota(jnp.int32, (B, B), 1)
    at_c = lax.broadcasted_iota(jnp.int32, (B, B), 0)
    same = jnp.where((key_c == key_r) & (at_c < at_r), 1, 0)
    less = jnp.where(key_c < key_r, 1, 0)
    more = jnp.sum(same, axis=0, keepdims=True)
    rank = more + jnp.sum(less, axis=0, keepdims=True)
    code = rank * 2 + jnp.where(more > 0, 1, 0)
    code_c = jnp.broadcast_to(code, (B, B)).T
    hit = (code_c >> 1) == at_r
    place = (at_c & (NC - 1)) * SLOTS + (at_c >> 5)
    table[0:1, :] = jnp.sum(jnp.where(hit, place, 0), axis=0, keepdims=True)
    table[1:2, :] = jnp.sum(jnp.where(hit, code_c & 1, 0), axis=0, keepdims=True)
    table[2:3, :] = key
    upto = jnp.sum(jnp.where(key_c <= at_r, 1, 0), axis=0, keepdims=True)
    some = jnp.sum(jnp.where(key_c == at_r, 1, 0), axis=0, keepdims=True)
    table[3:4, :] = jnp.where(some > 0, upto - 1, NB)
    table[4:8, :] = jnp.zeros((4, B), jnp.int32)
    to_idx = pltpu.make_async_copy(table, idx, sem_a.at[7])
    to_idx.start()

    def multiply(j):
        prod[pl.ds(j * SLOTS, SLOTS)] = jnp.dot(
            adj[j], panel[j], preferred_element_type=F32
        ).reshape(SLOTS, B, F)

    for cp in loads:
        cp.wait()
    multiply(me)

    for dz in (1, 3, 2):
        j = node(0, dz, core)
        spread(j, sib).wait_recv()
        for d in (1, 3, 2):
            send(spread(j, to_x(d)))
        send(spread(j, sib, None, e_r.at[NC + dz]))
        multiply(j)

    def from_x(dz, t, carry):
        j = node(ring4(t), dz, core)
        spread(j, sib).wait_recv()
        send(spread(j, sib, None, e_r.at[NC + dz]))
        multiply(j)
        return carry

    def from_sib(dz, t, carry):
        multiply(node(t, dz, 1 - core))
        return carry

    for dz in (0, 1, 3, 2):
        lax.fori_loop(0, 3, functools.partial(from_x, dz), 0)
    for dz in (0, 1, 3, 2):
        arrived(panel.at[pl.ds(0, NX)], e_r.at[NC + dz])
        lax.fori_loop(0, NX, functools.partial(from_sib, dz), 0)
    to_idx.wait()

    def segment(i, total):
        total = prod[idx[0, i]] + total * idx[1, i].astype(F32)
        seg[i] = total
        return total

    lax.fori_loop(0, NB, segment, jnp.zeros((B, F), F32), unroll=8)

    order = (4, 3, 5, 2, 6, 1, 7, 0)

    def part(half, d):
        return seg[idx[3, half * NY + wrap(y + d, NY)]]

    def zcopy(d):
        return remote(zs.at[d], zr.at[d], out.at[1], z_r.at[d], mate)

    def ycopy(d):
        return remote(ys.at[d], yr.at[d], out.at[2], y_r.at[0], to_y(d))

    for d in order:
        zs[d] = part(1 - zl, d).astype(BF)
        send(zcopy(d))
    for d in order[:-1]:
        zcopy(d).wait_recv()
        ys[d] = (part(zl, d) + zr[d].astype(F32)).astype(BF)
        send(ycopy(d))
    zcopy(0).wait_recv()
    total = part(zl, 0) + zr[0].astype(F32)
    arrived(yr.at[pl.ds(1, NY - 1)], y_r.at[0])
    for d in range(1, NY):
        total = total + yr[d].astype(F32)
    aggregate = total.astype(BF)

    weight = wgt[...]
    pre = jnp.dot(aggregate, weight, preferred_element_type=F32)
    s = 1.0 / (1.0 + jnp.exp(-pre))
    dpre = (cot[...].astype(F32) * (s * (1.0 + pre * (1.0 - s)))).astype(BF)
    dt[...] = lax.dot_general(
        weight, dpre, (((1,), (1,)), ((), ())), preferred_element_type=F32
    ).astype(BF)

    def share(k, where, src=None, sem=None):
        return remote(
            gt.at[k] if src is None else src, gt.at[k], out.at[3],
            g_r.at[k] if sem is None else sem, where,
        )

    send(share(col, mate, dt, g_r.at[BR]))
    for d in (1, 7, 2, 6, 3, 5, 4):
        send(share(col, to_y(d), dt))
    gt[col] = dt[...]

    grad_w = lax.dot_general(
        aggregate, dpre, (((0,), (0,)), ((), ())), preferred_element_type=F32
    )
    for c in range(2):
        lw[c] = grad_w[:, c * 128 : (c + 1) * 128].reshape(BR, 8, 128)
    chip = lax.div(row, 2)

    def w_half():
        return remote(lw.at[1 - core], lr, out.at[7], w_r.at[0], sib)

    def w_to_col():
        arrived(lr, w_r.at[0])
        ws[...] = lw[core] + lr[...]
        for d in range(1, BR):
            k = wrap(col + d, BR)
            send(remote(ws.at[k], wr.at[col], out.at[8], w_r.at[1], (row, k)))
        wr[col] = ws[col]

    def w_to_plane():
        arrived(wr.at[pl.ds(0, 15)], w_r.at[1])
        pr[chip] = jnp.sum(wr[...], axis=0)
        for d in range(1, 16):
            q = wrap(chip + d, 16)
            send(remote(pr.at[chip], pr.at[chip], out.at[9], w_r.at[2], (q * 2 + core, col)))

    def w_from_plane():
        arrived(pr.at[pl.ds(0, 15)], w_r.at[2])
        wg[core, col] = jnp.sum(pr[...], axis=0)
        for d in range(1, BR):
            k = wrap(col + d, BR)
            send(remote(wg.at[core, col], wg.at[core, col], out.at[10], w_r.at[3], (row, k)))

    def w_last():
        return remote(wg.at[core], wg.at[core], out.at[11], w_r.at[4], sib)

    def w_to_sib():
        arrived(wg.at[core, pl.ds(0, 15)], w_r.at[3])
        send(w_last())

    send(w_half())
    for n, d in enumerate((1, 7, 2, 6, 3, 5, 4)):
        k = zl * NY + wrap(y + d, NY)
        share(k, mate).wait_recv()
        send(share(k, mate, None, g_r.at[BR]))
        if n == 1:
            w_to_col()

    arrived(gt.at[pl.ds(0, NY)], g_r.at[BR])
    def column_grad(j):
        picked = jnp.concatenate([gt[idx[2, q * NC + j]] for q in range(SLOTS)], axis=1)
        return jnp.dot(picked, adj[j], preferred_element_type=F32)

    def ccopy(t):
        return remote(cs.at[t], cr.at[t], out.at[4], c_r.at[t], sib)

    def xcopy(t, d):
        return remote(xs.at[t], xr.at[t], out.at[5], x_r.at[t // NX], to_x(d))

    def produce(dz, dx):
        t = dz * NX + dx
        cs[t] = column_grad(node(dx, dz, 1 - core)).astype(BF)
        send(ccopy(t))
        keep[t] = column_grad(node(dx, dz, core))

    def pass_on(dz, dx):
        t = dz * NX + dx
        ccopy(t).wait_recv()
        both = keep[t] + cr[t].astype(F32)
        if dx == 0:
            keep[t] = both
        else:
            xs[t] = both.astype(BF)
            send(xcopy(t, dx))

    steps = [(dz, dx) for dz in (2, 1, 3, 0) for dx in (2, 1, 3, 0)]
    lag = 4
    for n in range(len(steps) + lag):
        if n < len(steps):
            produce(*steps[n])
        if n >= lag:
            pass_on(*steps[n - lag])
        if n == 3:
            w_to_plane()
        if n == 15:
            w_from_plane()

    def hcopy(dz):
        return remote(hs.at[dz], hr.at[dz], out.at[6], h_r.at[0], to_h(dz))

    def over_x(dz):
        acc = keep[dz * NX]
        arrived(xr.at[pl.ds(dz * NX + 1, NX - 1)], x_r.at[dz])
        for dx in (1, 2, 3):
            acc = acc + xr[dz * NX + dx].astype(F32)
        return acc

    for dz in (2, 1):
        hs[dz] = over_x(dz).astype(BF)
        send(hcopy(dz))
    hs[3] = over_x(3).astype(BF)
    send(hcopy(3))

    w_to_sib()
    acc = over_x(0)
    arrived(hr.at[pl.ds(1, NZ - 1)], h_r.at[0])
    for dz in (1, 2, 3):
        acc = acc + hr[dz].astype(F32)
    gout[...] = acc.T.astype(BF)

    w_last().wait_recv()
    for c in range(2):
        gw_out[:, c * 128 : (c + 1) * 128] = wg[c].reshape(F, 128)
    finish()


def body(embeddings, weight, cotangent, adj_blocks, block_rows, block_counts):
    adj = adj_blocks.reshape(NC, SLOTS * B, B)
    v = pltpu.VMEM
    dma = pltpu.SemaphoreType.DMA
    vmem = pl.BlockSpec(memory_space=pltpu.VMEM)
    hbm = pl.BlockSpec(memory_space=pltpu.HBM)
    tile = (B, F)
    wt = (8, 128)
    return pl.pallas_call(
        kernel,
        out_shape=(
            jax.ShapeDtypeStruct((B, F), BF),
            jax.ShapeDtypeStruct((F, HID), F32),
        ),
        in_specs=[hbm] * 6,
        out_specs=(vmem, vmem),
        scratch_shapes=[
            v((SLOTS, NC), jnp.int32), v((1, NC), jnp.int32),
            v((8, B), jnp.int32), v((8, B), jnp.int32),
            pltpu.SMEM((8, B), jnp.int32),
            v(tile, BF), v((F, HID), BF), v((B, HID), BF),
            v((NC, SLOTS * B, B), BF),
            v((NC,) + tile, BF),
            v((NB,) + tile, F32),
            v((NB + 1,) + tile, F32),
            v((NY,) + tile, BF), v((NY,) + tile, BF),
            v((NY,) + tile, BF), v((NY,) + tile, BF),
            v(tile, BF),
            v((BR + 1,) + tile, BF),
            v((16,) + tile, BF), v((16,) + tile, BF),
            v((16,) + tile, F32),
            v((16,) + tile, BF), v((16,) + tile, BF),
            v((NZ,) + tile, BF), v((NZ,) + tile, BF),
            v((2, BR) + wt, F32), v((BR,) + wt, F32),
            v((BR,) + wt, F32), v((BR,) + wt, F32),
            v((16,) + wt, F32), v((2, BR) + wt, F32),
            dma((10,)), dma((12,)), dma((NC + NZ,)), dma((NY,)), dma((1,)), dma((BR + 1,)),
            dma((16,)), dma((NZ,)), dma((1,)), dma((5,)),
        ],
        compiler_params=pltpu.CompilerParams(
            collective_id=0, has_side_effects=True, vmem_limit_bytes=VMEM_LIMIT
        ),
    )(*[
        pltpu.with_memory_space_constraint(a, pltpu.HBM)
        for a in (block_rows[0].T, block_counts, embeddings, weight, cotangent, adj)
    ])


def solution(mesh):
    return jax.shard_map(
        body,
        mesh=mesh,
        in_specs=(
            P(("col", "row"), None),
            P(),
            P(("row", "col"), None),
            P("row", "col", None, None, None),
            P("row", "col", None),
            P("row", "col"),
        ),
        out_specs=(P(("col", "row"), None), P()),
        check_vma=False,
    )
```

```python
import functools

import jax
import jax.numpy as jnp
from jax import lax
from jax.experimental import pallas as pl
from jax.experimental.pallas import tpu as pltpu
from jax.sharding import PartitionSpec as P

MESH = pl.DeviceIdType.MESH
BR = 16
NX, NZ, NY, NC = 4, 4, 8, 32
SLOTS = 4
VMEM_LIMIT = 40 * 2**20
B = 128
F = 128
HID = 256
NB = NC * SLOTS
BF = jnp.bfloat16
F32 = jnp.float32


def ring4(t):
    return 1 + 2 * t - 3 * lax.div(t, 2)


def wrap(a, n):
    return lax.rem(a, n)


def kernel(
    rows_hbm, counts_hbm, emb_hbm, wgt_hbm, cot_hbm, adj_hbm, gout, gw_out,
    rows_in, counts_in, wide, table, idx, emb, wgt, cot,
    adj, panel, prod, seg, zs, zr, ys, yr, dt, gt, cs, cr, keep, xs, xr, hs, hr,
    lw, lr, ws, wr, pr, wg,
    sem_a, out, e_r, z_r, y_r, g_r, c_r, x_r, h_r, w_r,
):
    row = lax.axis_index("row")
    col = lax.axis_index("col")
    x, zh, core = lax.div(row, 8), wrap(lax.div(row, 2), NZ), wrap(row, 2)
    zl, y = lax.div(col, NY), wrap(col, NY)

    def to_x(d):
        return ((wrap(x + d, NX) * NZ + zh) * 2 + core, col)

    def to_h(d):
        return ((x * NZ + wrap(zh + d, NZ)) * 2 + core, col)

    def to_y(d):
        return (row, zl * NY + wrap(y + d, NY))

    sib = ((x * NZ + zh) * 2 + 1 - core, col)
    mate = (row, (1 - zl) * NY + y)

    def node(dx, dz, c):
        return (wrap(x + dx, NX) * NZ + wrap(zh + dz, NZ)) * 2 + c

    def remote(src, dst, s, r, where):
        return pltpu.make_async_remote_copy(
            src_ref=src, dst_ref=dst, send_sem=s, recv_sem=r, device_id=where, device_id_type=MESH
        )

    def send(cp):
        cp.start()

    def arrived(ref, sem):
        remote(ref, ref, out.at[0], sem, sib).wait_recv()

    def finish():
        groups = (
            panel.at[pl.ds(0, 31)], zs, ys.at[pl.ds(0, 7)], gt.at[pl.ds(0, 15)], cs,
            xs.at[pl.ds(0, 12)], hs.at[pl.ds(0, 3)], lw.at[0], ws.at[pl.ds(0, 15)],
            pr.at[pl.ds(0, 15)], wg.at[0, pl.ds(0, 15)], wg.at[0],
        )
        for n, ref in enumerate(groups):
            remote(ref, ref, out.at[n], out.at[n], sib).wait_send()

    own_in = pltpu.make_async_copy(emb_hbm, emb, sem_a.at[4])
    own_in.start()
    barrier = pltpu.get_barrier_semaphore()
    peers = [to_h(d) for d in (2, 1, 3)] + [to_y(d) for d in (4, 3, 5, 2, 6)]
    peers += [to_x(d) for d in (2, 1, 3)] + [to_y(d) for d in (1, 7)] + [mate, sib]
    for peer in peers:
        pl.semaphore_signal(barrier, inc=1, device_id=peer, device_id_type=MESH)
    plan_in = [
        pltpu.make_async_copy(rows_hbm, rows_in, sem_a.at[8]),
        pltpu.make_async_copy(counts_hbm, counts_in, sem_a.at[9]),
    ]
    for cp in plan_in:
        cp.start()
    loads = [
        pltpu.make_async_copy(adj_hbm.at[pl.ds(8 * q, 8)], adj.at[pl.ds(8 * q, 8)], sem_a.at[q])
        for q in range(4)
    ]
    loads.append(pltpu.make_async_copy(wgt_hbm, wgt, sem_a.at[5]))
    loads.append(pltpu.make_async_copy(cot_hbm, cot, sem_a.at[6]))
    for cp in loads:
        cp.start()

    me = node(0, 0, core)
    gt[BR] = jnp.zeros((B, B), BF)
    seg[NB] = jnp.zeros((B, F), F32)
    own_in.wait()
    pl.semaphore_wait(barrier, len(peers))

    def spread(j, where, src=None, sem=None):
        return remote(
            panel.at[j] if src is None else src, panel.at[j], out.at[0],
            e_r.at[j] if sem is None else sem, where,
        )

    for d in (1, 3, 2):
        send(spread(me, to_h(d), emb))
    for d in (1, 3, 2):
        send(spread(me, to_x(d), emb))
    send(spread(me, sib, emb, e_r.at[NC]))
    panel[me] = emb[...]

    for cp in plan_in:
        cp.wait()
    wide[...] = jnp.zeros((8, B), jnp.int32)
    wide[0:SLOTS, 0:NC] = rows_in[...]
    wide[SLOTS : SLOTS + 1, 0:NC] = counts_in[...]
    lane = lax.broadcasted_iota(jnp.int32, (1, B), 1)
    limit = wide[SLOTS : SLOTS + 1, :]
    key = jnp.zeros((1, B), jnp.int32)
    for q in range(SLOTS):
        mine = jnp.where(limit > q, wide[q : q + 1, :], BR)
        mine = jnp.where(lane < NC, mine, 0)
        key = key + (pltpu.roll(mine, q * NC, 1) if q else mine)
    key_r = jnp.broadcast_to(key, (B, B))
    key_c = key_r.T
    at_r = lax.broadcasted_iota(jnp.int32, (B, B), 1)
    at_c = lax.broadcasted_iota(jnp.int32, (B, B), 0)
    same = jnp.where((key_c == key_r) & (at_c < at_r), 1, 0)
    less = jnp.where(key_c < key_r, 1, 0)
    more = jnp.sum(same, axis=0, keepdims=True)
    rank = more + jnp.sum(less, axis=0, keepdims=True)
    code = rank * 2 + jnp.where(more > 0, 1, 0)
    code_c = jnp.broadcast_to(code, (B, B)).T
    hit = (code_c >> 1) == at_r
    place = (at_c & (NC - 1)) * SLOTS + (at_c >> 5)
    table[0:1, :] = jnp.sum(jnp.where(hit, place, 0), axis=0, keepdims=True)
    table[1:2, :] = jnp.sum(jnp.where(hit, code_c & 1, 0), axis=0, keepdims=True)
    table[2:3, :] = key
    upto = jnp.sum(jnp.where(key_c <= at_r, 1, 0), axis=0, keepdims=True)
    some = jnp.sum(jnp.where(key_c == at_r, 1, 0), axis=0, keepdims=True)
    table[3:4, :] = jnp.where(some > 0, upto - 1, NB)
    table[4:8, :] = jnp.zeros((4, B), jnp.int32)
    to_idx = pltpu.make_async_copy(table, idx, sem_a.at[7])
    to_idx.start()

    def multiply(j):
        prod[pl.ds(j * SLOTS, SLOTS)] = jnp.dot(
            adj[j], panel[j], preferred_element_type=F32
        ).reshape(SLOTS, B, F)

    for cp in loads:
        cp.wait()
    multiply(me)

    for dz in (1, 3, 2):
        j = node(0, dz, core)
        spread(j, sib).wait_recv()
        for d in (1, 3, 2):
            send(spread(j, to_x(d)))
        send(spread(j, sib, None, e_r.at[NC + dz]))
        multiply(j)

    def from_x(dz, t, carry):
        j = node(ring4(t), dz, core)
        spread(j, sib).wait_recv()
        send(spread(j, sib, None, e_r.at[NC + dz]))
        multiply(j)
        return carry

    def from_sib(dz, t, carry):
        multiply(node(t, dz, 1 - core))
        return carry

    for dz in (0, 1, 3, 2):
        lax.fori_loop(0, 3, functools.partial(from_x, dz), 0)
    for dz in (0, 1, 3, 2):
        arrived(panel.at[pl.ds(0, NX)], e_r.at[NC + dz])
        lax.fori_loop(0, NX, functools.partial(from_sib, dz), 0)
    to_idx.wait()

    def segment(i, total):
        total = prod[idx[0, i]] + total * idx[1, i].astype(F32)
        seg[i] = total
        return total

    lax.fori_loop(0, NB, segment, jnp.zeros((B, F), F32), unroll=16)

    order = (4, 3, 5, 2, 6, 1, 7, 0)

    def part(half, d):
        return seg[idx[3, half * NY + wrap(y + d, NY)]]

    def zcopy(d):
        return remote(zs.at[d], zr.at[d], out.at[1], z_r.at[d], mate)

    def ycopy(d):
        return remote(ys.at[d], yr.at[d], out.at[2], y_r.at[0], to_y(d))

    for d in order:
        zs[d] = part(1 - zl, d).astype(BF)
        send(zcopy(d))
    for d in order[:-1]:
        zcopy(d).wait_recv()
        ys[d] = (part(zl, d) + zr[d].astype(F32)).astype(BF)
        send(ycopy(d))
    zcopy(0).wait_recv()
    total = part(zl, 0) + zr[0].astype(F32)
    arrived(yr.at[pl.ds(1, NY - 1)], y_r.at[0])
    for d in range(1, NY):
        total = total + yr[d].astype(F32)
    aggregate = total.astype(BF)

    weight = wgt[...]
    pre = jnp.dot(aggregate, weight, preferred_element_type=F32)
    s = 1.0 / (1.0 + jnp.exp(-pre))
    dpre = (cot[...].astype(F32) * (s * (1.0 + pre * (1.0 - s)))).astype(BF)
    dt[...] = lax.dot_general(
        weight, dpre, (((1,), (1,)), ((), ())), preferred_element_type=F32
    ).astype(BF)

    def share(k, where, src=None, sem=None):
        return remote(
            gt.at[k] if src is None else src, gt.at[k], out.at[3],
            g_r.at[k] if sem is None else sem, where,
        )

    send(share(col, mate, dt, g_r.at[BR]))
    for d in (1, 7, 2, 6, 3, 5, 4):
        send(share(col, to_y(d), dt))
    gt[col] = dt[...]

    grad_w = lax.dot_general(
        aggregate, dpre, (((0,), (0,)), ((), ())), preferred_element_type=F32
    )
    for c in range(2):
        lw[c] = grad_w[:, c * 128 : (c + 1) * 128].reshape(BR, 8, 128)
    chip = lax.div(row, 2)

    def w_half():
        return remote(lw.at[1 - core], lr, out.at[7], w_r.at[0], sib)

    def w_to_col():
        arrived(lr, w_r.at[0])
        ws[...] = lw[core] + lr[...]
        for d in range(1, BR):
            k = wrap(col + d, BR)
            send(remote(ws.at[k], wr.at[col], out.at[8], w_r.at[1], (row, k)))
        wr[col] = ws[col]

    def w_to_plane():
        arrived(wr.at[pl.ds(0, 15)], w_r.at[1])
        pr[chip] = jnp.sum(wr[...], axis=0)
        for d in range(1, 16):
            q = wrap(chip + d, 16)
            send(remote(pr.at[chip], pr.at[chip], out.at[9], w_r.at[2], (q * 2 + core, col)))

    def w_from_plane():
        arrived(pr.at[pl.ds(0, 15)], w_r.at[2])
        wg[core, col] = jnp.sum(pr[...], axis=0)
        for d in range(1, BR):
            k = wrap(col + d, BR)
            send(remote(wg.at[core, col], wg.at[core, col], out.at[10], w_r.at[3], (row, k)))

    def w_last():
        return remote(wg.at[core], wg.at[core], out.at[11], w_r.at[4], sib)

    def w_to_sib():
        arrived(wg.at[core, pl.ds(0, 15)], w_r.at[3])
        send(w_last())

    send(w_half())
    for n, d in enumerate((1, 7, 2, 6, 3, 5, 4)):
        k = zl * NY + wrap(y + d, NY)
        share(k, mate).wait_recv()
        send(share(k, mate, None, g_r.at[BR]))
        if n == 1:
            w_to_col()

    arrived(gt.at[pl.ds(0, NY)], g_r.at[BR])
    def column_grad(j):
        picked = jnp.concatenate([gt[idx[2, q * NC + j]] for q in range(SLOTS)], axis=1)
        return jnp.dot(picked, adj[j], preferred_element_type=F32)

    def ccopy(t):
        return remote(cs.at[t], cr.at[t], out.at[4], c_r.at[t], sib)

    def xcopy(t, d):
        return remote(xs.at[t], xr.at[t], out.at[5], x_r.at[t // NX], to_x(d))

    def produce(dz, dx):
        t = dz * NX + dx
        cs[t] = column_grad(node(dx, dz, 1 - core)).astype(BF)
        send(ccopy(t))
        keep[t] = column_grad(node(dx, dz, core))

    def pass_on(dz, dx):
        t = dz * NX + dx
        ccopy(t).wait_recv()
        both = keep[t] + cr[t].astype(F32)
        if dx == 0:
            keep[t] = both
        else:
            xs[t] = both.astype(BF)
            send(xcopy(t, dx))

    steps = [(dz, dx) for dz in (2, 1, 3, 0) for dx in (2, 1, 3, 0)]
    lag = 4
    for n in range(len(steps) + lag):
        if n < len(steps):
            produce(*steps[n])
        if n >= lag:
            pass_on(*steps[n - lag])
        if n == 3:
            w_to_plane()
        if n == 15:
            w_from_plane()

    def hcopy(dz):
        return remote(hs.at[dz], hr.at[dz], out.at[6], h_r.at[0], to_h(dz))

    def over_x(dz):
        acc = keep[dz * NX]
        arrived(xr.at[pl.ds(dz * NX + 1, NX - 1)], x_r.at[dz])
        for dx in (1, 2, 3):
            acc = acc + xr[dz * NX + dx].astype(F32)
        return acc

    for dz in (2, 1):
        hs[dz] = over_x(dz).astype(BF)
        send(hcopy(dz))
    hs[3] = over_x(3).astype(BF)
    send(hcopy(3))

    w_to_sib()
    acc = over_x(0)
    arrived(hr.at[pl.ds(1, NZ - 1)], h_r.at[0])
    for dz in (1, 2, 3):
        acc = acc + hr[dz].astype(F32)
    gout[...] = acc.T.astype(BF)

    w_last().wait_recv()
    for c in range(2):
        gw_out[:, c * 128 : (c + 1) * 128] = wg[c].reshape(F, 128)
    finish()


def body(embeddings, weight, cotangent, adj_blocks, block_rows, block_counts):
    adj = adj_blocks.reshape(NC, SLOTS * B, B)
    v = pltpu.VMEM
    dma = pltpu.SemaphoreType.DMA
    vmem = pl.BlockSpec(memory_space=pltpu.VMEM)
    hbm = pl.BlockSpec(memory_space=pltpu.HBM)
    tile = (B, F)
    wt = (8, 128)
    return pl.pallas_call(
        kernel,
        out_shape=(
            jax.ShapeDtypeStruct((B, F), BF),
            jax.ShapeDtypeStruct((F, HID), F32),
        ),
        in_specs=[hbm] * 6,
        out_specs=(vmem, vmem),
        scratch_shapes=[
            v((SLOTS, NC), jnp.int32), v((1, NC), jnp.int32),
            v((8, B), jnp.int32), v((8, B), jnp.int32),
            pltpu.SMEM((8, B), jnp.int32),
            v(tile, BF), v((F, HID), BF), v((B, HID), BF),
            v((NC, SLOTS * B, B), BF),
            v((NC,) + tile, BF),
            v((NB,) + tile, F32),
            v((NB + 1,) + tile, F32),
            v((NY,) + tile, BF), v((NY,) + tile, BF),
            v((NY,) + tile, BF), v((NY,) + tile, BF),
            v(tile, BF),
            v((BR + 1,) + tile, BF),
            v((16,) + tile, BF), v((16,) + tile, BF),
            v((16,) + tile, F32),
            v((16,) + tile, BF), v((16,) + tile, BF),
            v((NZ,) + tile, BF), v((NZ,) + tile, BF),
            v((2, BR) + wt, F32), v((BR,) + wt, F32),
            v((BR,) + wt, F32), v((BR,) + wt, F32),
            v((16,) + wt, F32), v((2, BR) + wt, F32),
            dma((10,)), dma((12,)), dma((NC + NZ,)), dma((NY,)), dma((1,)), dma((BR + 1,)),
            dma((16,)), dma((NZ,)), dma((1,)), dma((5,)),
        ],
        compiler_params=pltpu.CompilerParams(
            collective_id=0, has_side_effects=True, vmem_limit_bytes=VMEM_LIMIT
        ),
    )(*[
        pltpu.with_memory_space_constraint(a, pltpu.HBM)
        for a in (block_rows[0].T, block_counts, embeddings, weight, cotangent, adj)
    ])


def solution(mesh):
    return jax.shard_map(
        body,
        mesh=mesh,
        in_specs=(
            P(("col", "row"), None),
            P(),
            P(("row", "col"), None),
            P("row", "col", None, None, None),
            P("row", "col", None),
            P("row", "col"),
        ),
        out_specs=(P(("col", "row"), None), P()),
        check_vma=False,
    )
```
